32 devices in a mesh: range: 8 (over z, y), doppler: 4 (over x, core).
Axes of the slice: x: 2, y: 2, z: 4, core: 2. Of those that a mesh axis runs over, the one named last changes fastest.
Arguments:
- snapshots: bfloat16 [32, 4096, 384], P(None, ('range', 'doppler')), may hold values from -24 to 24
- steering: bfloat16 [32, 384, 256], P(('range', 'doppler')), may hold values from -0.3125 to 0.3125
- train_list: int32 [32, 32], P(('range', 'doppler')), may hold values from 0 to 31, each once within a row
- train_count: int32 [32], P(('range', 'doppler')), may hold values from 10 to 32, as said below
Outputs:
- beam_output: bfloat16 [32, 4096, 256], P(None, ('range', 'doppler'))
The draws below stay inside these ranges and needn't reach their ends.
Inputs may be any that keep to these rules, and one draw needn't show every extreme that they name: `train_count`: some bin trains on all 32 blocks and some bin on 10.
All inputs are finite; a program needn't handle non-finite values.
Results may differ from the reference program's by a relative error of at most 0.0052.
Values may be sent and summed in bfloat16 or wider, within the bound.
No kernel may reach another device: no remote copies, remote signals or barrier semaphores. Data moves between devices by JAX's collectives and lax.ppermute only.
A program may use at most 128 MiB of HBM per device.

```python
import math
import jax
import jax.numpy as jnp
from jax import lax

DOF = 384
BEAMS = 256
BLOCK = 128
BINS = 32
NBLK = 32
GATES = 4096


def draw_snapshots(key, part):
    subkeys = jax.random.split(key, 5)
    block_total = GATES // BLOCK
    noise = jax.random.normal(subkeys[0], (BINS, GATES, DOF), jnp.float32)
    power = jnp.exp(jax.random.uniform(subkeys[1], (BINS, block_total), jnp.float32, math.log(0.4), math.log(4.0)))
    gains = jax.random.uniform(subkeys[2], (DOF,), jnp.float32, 0.5, 1.5)
    clutter = jax.random.normal(subkeys[3], (BINS, GATES), jnp.float32)
    pattern = jax.random.normal(subkeys[4], (BINS, DOF), jnp.float32) * 0.3
    level = jnp.repeat(power, BLOCK, axis=1, total_repeat_length=GATES)
    values = level[:, :, None] * (noise * gains[None, None, :] + clutter[:, :, None] * pattern[:, None, :])
    return jnp.clip(values, -24.0, 24.0).astype(jnp.bfloat16)


def draw_train_count(key, part):
    subkeys = jax.random.split(key, 2)
    block_total = GATES // BLOCK
    counts = jax.random.randint(subkeys[0], (BINS,), block_total // 3, block_total + 1)
    fullest = jax.random.randint(subkeys[1], (), 0, BINS)
    fewest = (fullest + BINS // 2) % BINS
    bin_ids = jnp.arange(BINS, dtype=jnp.int32)
    counts = jnp.where(bin_ids == fullest, block_total, counts)
    counts = jnp.where(bin_ids == fewest, block_total // 3, counts)
    return counts.astype(jnp.int32)


def block_scale(rng, extent, cuts, smallest, high):
    def one(dim, blocks):
        draws = jax.random.uniform(jax.random.fold_in(jax.random.fold_in(rng, 6), dim), (blocks,), jnp.float32, smallest / len(cuts), high / len(cuts))
        return jnp.repeat(jnp.exp(draws), extent[dim] // blocks).reshape((-1,) + (1,) * (len(extent) - dim - 1))

    level = one(*cuts[0])
    for cut in cuts[1:]:
        level = level * one(*cut)
    return level


def centred(rng, extent, scale, bound, shards=(), kind=jnp.bfloat16):
    loudness = block_scale(rng, extent, shards, -0.22, 0.18) if shards else 1.0
    values = jax.random.normal(rng, extent, jnp.float32) * scale * loudness
    return jnp.minimum(jnp.maximum(values, -bound), bound).astype(kind)


def setup_inputs(seed: int = 0) -> dict:
    arg_keys = jax.random.split(jax.random.key(seed), 5)
    snapshots = draw_snapshots(jax.random.fold_in(arg_keys[4], 71), 0)
    steering = centred(arg_keys[1], (BINS, DOF, BEAMS), DOF ** -0.5, 0.3125, ((0, 32),))
    train_list = jax.vmap(lambda own: jax.random.permutation(own, NBLK))(jax.random.split(arg_keys[2], BINS)).reshape((BINS, NBLK)).astype(jnp.int32)
    train_count = draw_train_count(jax.random.fold_in(arg_keys[4], 71), 0)
    return {"snapshots": snapshots, "steering": steering, "train_list": train_list, "train_count": train_count}


LOADING = 0.1

def cholesky_solve(factor, rhs_block):
    inner = lax.linalg.triangular_solve(factor, rhs_block, left_side=True, lower=True)
    return lax.linalg.triangular_solve(factor, inner, left_side=True, lower=True, transpose_a=True)

def one_bin(operands):
    snaps, steer, order_list, train_rows = operands
    block_total = order_list.shape[0]
    position = jnp.arange(block_total, dtype=jnp.int32)
    block_ids = jnp.arange(block_total, dtype=jnp.int32)
    matches = (order_list[:, None] == block_ids[None, :]) & (position[:, None] < train_rows)
    chosen = jnp.sum(matches.astype(jnp.int32), axis=0)
    blocks = snaps.reshape(block_total, BLOCK, DOF).astype(jnp.float32)
    masked = blocks * chosen.astype(jnp.float32)[:, None, None]
    gram_sum = jnp.einsum('nrd,nre->de', masked, blocks, precision=lax.Precision.HIGHEST)
    scale = (BLOCK * train_rows).astype(jnp.float32)
    covariance = gram_sum / scale + LOADING * jnp.eye(DOF, dtype=jnp.float32)
    factor = jnp.linalg.cholesky(covariance)
    steer_full = steer.astype(jnp.float32)
    solved = cholesky_solve(factor, steer_full)
    response = jnp.sum(steer_full * solved, axis=0)
    weights = (solved / response[None, :]).astype(jnp.bfloat16)
    return jnp.dot(snaps.astype(jnp.float32), weights.astype(jnp.float32), preferred_element_type=jnp.float32).astype(jnp.bfloat16)

def reference(snapshots, steering, train_list, train_count):
    return lax.map(one_bin, (snapshots, steering, train_list, train_count))
```

```python
import jax
import jax.numpy as jnp
from jax import lax
from jax.experimental import pallas as pl
from jax.experimental.pallas import tpu as pltpu
from jax.sharding import Mesh
from jax.sharding import PartitionSpec as P

BLOCK = 128
LOADING = 0.1
EDGE = 128
STEP = 16
INNER = ("inner", "doppler")


def selection(train_list, train_count):
    block_total = train_list.shape[1]
    position = lax.broadcasted_iota(jnp.int32, (1, block_total, 1), 1)
    block_ids = lax.broadcasted_iota(jnp.int32, (1, 1, block_total), 2)
    matches = (train_list[:, :, None] == block_ids) & (position < train_count[:, None, None])
    return jnp.sum(matches.astype(jnp.int32), axis=1)


def partial_gram(blocks, chosen):
    masked = blocks * chosen.astype(blocks.dtype)[:, None, None]
    flat = (blocks.shape[0] * blocks.shape[1], blocks.shape[2])
    return lax.dot_general(
        masked.reshape(flat), blocks.reshape(flat), (((0,), (0,)), ((), ())),
        preferred_element_type=jnp.float32,
    )


def pack(gram):
    size = gram.shape[0]
    return jnp.concatenate([gram[i : i + 128, i:] for i in range(0, size, 128)], axis=1)


def fine(a, b, dims=(((1,), (0,)), ((), ()))):
    return lax.dot_general(
        a, b, dims, precision=lax.Precision.HIGHEST, preferred_element_type=jnp.float32
    )


def thirds(x):
    hi = x.astype(jnp.bfloat16)
    rest = x - hi.astype(jnp.float32)
    mid = rest.astype(jnp.bfloat16)
    low = (rest - mid.astype(jnp.float32)).astype(jnp.bfloat16)
    return hi, mid, low


def outer(a, b):
    ah, am, al = thirds(a)
    bh, bm, bl = thirds(b)
    left = jnp.concatenate([ah, ah, ah, am, am, al], axis=0)
    right = jnp.concatenate([bh, bm, bl, bh, bm, bh], axis=0)
    return lax.dot_general(
        left, right, (((0,), (0,)), ((), ())), preferred_element_type=jnp.float32
    )


def negative_inverse(strips):
    sub = lax.broadcasted_iota(jnp.int32, (STEP, EDGE), 0)
    lane = lax.broadcasted_iota(jnp.int32, (STEP, EDGE), 1)
    full = (STEP, EDGE)
    for p in range(EDGE // STEP):
        rows = strips[p]
        at = p * STEP
        inside = (lane >= at) & (lane < at + STEP)
        swept = jnp.where(inside, jnp.where(lane == sub + at, -1.0, 0.0), rows)
        cols = [jnp.broadcast_to(rows[:, at + i : at + i + 1], full) for i in range(STEP)]
        solved = swept
        for k in range(STEP):
            here = sub == k
            inv = 1.0 / jnp.broadcast_to(cols[k][k : k + 1], full)
            factor = jnp.where(here, 1.0, -cols[k])
            solved = jnp.where(here, 0.0, solved) + factor * (
                jnp.broadcast_to(solved[k : k + 1], full) * inv
            )
            for i in range(k + 1, STEP):
                cols[i] = jnp.where(here, 0.0, cols[i]) + factor * (
                    jnp.broadcast_to(cols[i][k : k + 1], full) * inv
                )
        change = outer(swept, solved)
        strips = [
            (jnp.zeros(full, jnp.float32) if q == p else jnp.where(inside, 0.0, strips[q]))
            - change[q * STEP : (q + 1) * STEP]
            for q in range(EDGE // STEP)
        ]
    return jnp.concatenate(strips, axis=0)


def solve_kernel(count_ref, own_ref, other_ref, steer_ref, out_ref, work):
    size = own_ref.shape[0]
    parts = size // EDGE
    inv_scale = 1.0 / (BLOCK * count_ref[0]).astype(jnp.float32)
    at = 0
    for i in range(parts):
        width = size - i * EDGE
        rows = pl.ds(i * EDGE, EDGE)
        strip = (own_ref[rows, pl.ds(i * EDGE, width)] + other_ref[:, pl.ds(at, width)]) * inv_scale
        r = lax.broadcasted_iota(jnp.int32, (EDGE, width), 0)
        c = lax.broadcasted_iota(jnp.int32, (EDGE, width), 1)
        work[rows, pl.ds(i * EDGE, width)] = strip + jnp.where(r == c, LOADING, 0.0)
        at += width
    beams = steer_ref.shape[1]
    work[:, pl.ds(size, beams)] = steer_ref[...].astype(jnp.float32)
    total = size + beams
    made = []
    for i in range(parts):
        rows = pl.ds(i * EDGE, EDGE)
        strips = [
            work[pl.ds(i * EDGE + q * STEP, STEP), pl.ds(i * EDGE, EDGE)]
            for q in range(EDGE // STEP)
        ]
        minus = negative_inverse(strips)
        right = work[rows, pl.ds((i + 1) * EDGE, total - (i + 1) * EDGE)]
        p = -fine(minus, right)
        made.append(p)
        for j in range(i + 1, parts):
            lhs = work[rows, pl.ds(j * EDGE, EDGE)]
            cut = p[:, (j - i - 1) * EDGE :]
            span = pl.ds(j * EDGE, total - j * EDGE)
            target = pl.ds(j * EDGE, EDGE)
            work[target, span] = work[target, span] - fine(lhs, cut, (((0,), (0,)), ((), ())))
    found = [None] * parts
    for i in reversed(range(parts)):
        x = made[i][:, (parts - i - 1) * EDGE :]
        for j in range(i + 1, parts):
            x = x - fine(made[i][:, (j - i - 1) * EDGE : (j - i) * EDGE], found[j])
        found[i] = x
    response = 0.0
    for i in range(parts):
        steer = steer_ref[pl.ds(i * EDGE, EDGE), :].astype(jnp.float32)
        response = response + jnp.sum(steer * found[i], axis=0, keepdims=True)
    for i in range(parts):
        out_ref[pl.ds(i * EDGE, EDGE), :] = (found[i] / response).astype(out_ref.dtype)


def make_weights(count, own, other, steering):
    size, beams = steering.shape
    vmem = pl.BlockSpec(memory_space=pltpu.VMEM)
    return pl.pallas_call(
        solve_kernel,
        out_shape=jax.ShapeDtypeStruct((size, beams), jnp.bfloat16),
        in_specs=[pl.BlockSpec(memory_space=pltpu.SMEM), vmem, vmem, vmem],
        out_specs=vmem,
        scratch_shapes=[pltpu.VMEM((size, size + beams), jnp.float32)],
        compiler_params=pltpu.CompilerParams(vmem_limit_bytes=32 * 1024 * 1024),
        cost_estimate=pl.CostEstimate(flops=10**9, bytes_accessed=2 * 10**6, transcendentals=0),
    )(count, own, other, steering)


def body(halves, snapshots, steering, train_list, train_count):
    bin_total, gate_rows, channels = snapshots.shape
    half = lax.axis_index("half")
    group = bin_total // halves
    peers = [(0, 1), (1, 0)]
    by_half = snapshots.reshape(halves, group, gate_rows, channels)

    def fetch(which):
        out = lax.dynamic_index_in_dim(by_half, which, 0, keepdims=False)
        return lax.all_to_all(out, INNER, split_axis=0, concat_axis=0, tiled=True)

    chosen_all = selection(train_list, train_count)[0].reshape(halves, group)
    own_chosen = lax.dynamic_index_in_dim(chosen_all, half, 0, keepdims=False)
    give_chosen = lax.dynamic_index_in_dim(chosen_all, 1 - half, 0, keepdims=False)
    other_chosen = lax.ppermute(give_chosen, "half", peers)

    other_blocks = fetch(1 - half)
    other_gram = partial_gram(other_blocks, other_chosen)
    arrived = lax.ppermute(pack(other_gram), "half", peers)
    own_blocks = fetch(half)
    own_gram = partial_gram(own_blocks, own_chosen)
    weights = make_weights(train_count, own_gram, arrived, steering[0])
    other_weights = lax.ppermute(weights, "half", peers)

    def beams(blocks, w):
        made = jnp.einsum("ngd,de->nge", blocks, w, preferred_element_type=jnp.float32)
        return lax.all_to_all(
            made.astype(jnp.bfloat16), INNER, split_axis=0, concat_axis=0, tiled=True
        )

    own_out = beams(own_blocks, weights)
    other_out = beams(other_blocks, other_weights)
    first = half == 0
    return jnp.concatenate(
        [jnp.where(first, own_out, other_out), jnp.where(first, other_out, own_out)], axis=0
    )


def solution(mesh):
    ranges, dopplers = mesh.devices.shape
    halves = 2
    cut = Mesh(
        mesh.devices.reshape(halves, ranges // halves, dopplers), ("half", "inner", "doppler")
    )
    every = ("half", "inner", "doppler")

    def run(*args):
        return body(halves, *args)

    return jax.shard_map(
        run,
        mesh=cut,
        in_specs=(P(None, every, None), P(every, None, None), P(every, None), P(every)),
        out_specs=P(None, every, None),
        check_vma=False,
    )
```

```python
import jax
import jax.numpy as jnp
from jax import lax
from jax.experimental import pallas as pl
from jax.experimental.pallas import tpu as pltpu
from jax.sharding import Mesh
from jax.sharding import PartitionSpec as P

BLOCK = 128
LOADING = 0.1
EDGE = 128
STEP = 16
INNER = ("inner", "doppler")


def gram_kernel(base_ref, list_ref, count_ref, blocks_ref, out_ref, chosen):
    step = pl.program_id(0)
    count, _, rows, size = blocks_ref.shape

    @pl.when(step == 0)
    def _():
        for p in range(list_ref.shape[1]):
            chosen[list_ref[0, p]] = (p < count_ref[0]).astype(jnp.int32)

    first = base_ref[0] + step * count
    every = [blocks_ref[n, 0] for n in range(count)]
    kept = [
        jnp.where(chosen[first + n] > 0, x, jnp.zeros_like(x)) for n, x in enumerate(every)
    ]
    every = jnp.concatenate(every, axis=0)
    kept = jnp.concatenate(kept, axis=0)
    def product(lo, hi):
        return lax.dot_general(
            kept[:, lo:hi], every[:, lo:], (((0,), (0,)), ((), ())),
            preferred_element_type=jnp.float32,
        )

    at = 0
    for lo in range(0, size, 2 * EDGE):
        hi = min(lo + 2 * EDGE, size)
        part = product(lo, hi)
        for i in range(lo, hi, EDGE):
            width = size - i
            out_ref[:, pl.ds(at, width)] = part[i - lo : i - lo + EDGE, i - lo :]
            at += width


def partial_gram(base, lists, counts, blocks, which, chunks=1):
    group, _, rows, size = blocks.shape
    parts = size // EDGE
    smem = pl.BlockSpec(memory_space=pltpu.SMEM)
    wide = EDGE * parts * (parts + 1) // 2
    return pl.pallas_call(
        gram_kernel,
        out_shape=jax.ShapeDtypeStruct((EDGE, wide), jnp.float32),
        grid=(chunks,),
        in_specs=[smem, smem, smem, pl.BlockSpec((group // chunks, 1, rows, size), lambda i: (i, which, 0, 0))],
        out_specs=pl.BlockSpec((EDGE, wide), lambda i: (0, 0)),
        scratch_shapes=[pltpu.SMEM((lists.shape[1],), jnp.int32)],
        compiler_params=pltpu.CompilerParams(vmem_limit_bytes=16 * 1024 * 1024),
        cost_estimate=pl.CostEstimate(
            flops=2 * group * rows * size * size, bytes_accessed=2 * group * rows * size, transcendentals=0
        ),
    )(base, lists, counts, blocks)


def fine(a, b, dims=(((1,), (0,)), ((), ()))):
    return lax.dot_general(
        a, b, dims, precision=lax.Precision.HIGHEST, preferred_element_type=jnp.float32
    )


def thirds(x):
    hi = x.astype(jnp.bfloat16)
    rest = x - hi.astype(jnp.float32)
    mid = rest.astype(jnp.bfloat16)
    low = (rest - mid.astype(jnp.float32)).astype(jnp.bfloat16)
    return hi, mid, low


def outer(a, b):
    ah, am, al = thirds(a)
    bh, bm, bl = thirds(b)
    left = jnp.concatenate([ah, ah, ah, am, am, al], axis=0)
    right = jnp.concatenate([bh, bm, bl, bh, bm, bh], axis=0)
    return lax.dot_general(
        left, right, (((0,), (0,)), ((), ())), preferred_element_type=jnp.float32
    )


def eliminate(rows, cols):
    full = (STEP, EDGE)
    sub = lax.broadcasted_iota(jnp.int32, full, 0)

    def row(x, k):
        return jnp.broadcast_to(x[k : k + 1], full)

    cols = list(cols)
    for k in range(0, STEP, 2):
        one, two = sub == k, sub == k + 1
        here = one | two
        a, b, c = row(cols[k], k), row(cols[k + 1], k), row(cols[k + 1], k + 1)
        inv = 1.0 / (a * c - b * b)
        first = jnp.where(one, 1.0, jnp.where(two, 0.0, -cols[k]))
        second = jnp.where(two, 1.0, jnp.where(one, 0.0, -cols[k + 1]))

        def step(x):
            r, s = row(x, k), row(x, k + 1)
            up = (c * r - b * s) * inv
            down = (a * s - b * r) * inv
            return (jnp.where(here, 0.0, x) + first * up) + second * down

        for i in range(k + 2, STEP):
            cols[i] = step(cols[i])
        rows = step(rows)
    return rows


def negative_inverse(strips):
    full = (STEP, EDGE)
    panels = EDGE // STEP
    sub = lax.broadcasted_iota(jnp.int32, full, 0)
    lane = lax.broadcasted_iota(jnp.int32, full, 1)

    def spread(x, at):
        return [jnp.broadcast_to(x[:, at + i : at + i + 1], full) for i in range(STEP)]

    rows = strips[0]
    for p in range(panels):
        at = p * STEP
        inside = (lane >= at) & (lane < at + STEP)
        swept = jnp.where(inside, jnp.where(lane == sub + at, -1.0, 0.0), rows)
        weights = spread(strips[p + 1], at) if p + 1 < panels else None
        solved = eliminate(swept, spread(rows, at))
        if weights is not None:
            terms = [w * jnp.broadcast_to(solved[k : k + 1], full) for k, w in enumerate(weights)]
            while len(terms) > 1:
                terms = [x + y for x, y in zip(terms[::2], terms[1::2])]
            rows = jnp.where(inside, 0.0, strips[p + 1]) - terms[0]
        change = outer(swept, solved)
        strips = [
            rows
            if q == p + 1
            else (jnp.zeros(full, jnp.float32) if q == p else jnp.where(inside, 0.0, strips[q]))
            - change[q * STEP : (q + 1) * STEP]
            for q in range(panels)
        ]
    return jnp.concatenate(strips, axis=0)


def solve_kernel(count_ref, own_ref, other_ref, steer_ref, out_ref, work):
    size = steer_ref.shape[0]
    parts = size // EDGE
    inv_scale = 1.0 / (BLOCK * count_ref[0]).astype(jnp.float32)
    at = 0
    for i in range(parts):
        width = size - i * EDGE
        rows = pl.ds(i * EDGE, EDGE)
        strip = (own_ref[:, pl.ds(at, width)] + other_ref[:, pl.ds(at, width)]) * inv_scale
        r = lax.broadcasted_iota(jnp.int32, (EDGE, width), 0)
        c = lax.broadcasted_iota(jnp.int32, (EDGE, width), 1)
        work[rows, pl.ds(i * EDGE, width)] = strip + jnp.where(r == c, LOADING, 0.0)
        at += width
    beams = steer_ref.shape[1]
    work[:, pl.ds(size, beams)] = steer_ref[...].astype(jnp.float32)
    total = size + beams
    made = []
    for i in range(parts):
        rows = pl.ds(i * EDGE, EDGE)
        strips = [
            work[pl.ds(i * EDGE + q * STEP, STEP), pl.ds(i * EDGE, EDGE)]
            for q in range(EDGE // STEP)
        ]
        minus = negative_inverse(strips)
        right = work[rows, pl.ds((i + 1) * EDGE, total - (i + 1) * EDGE)]
        p = -fine(minus, right)
        made.append(p)
        for j in range(i + 1, parts):
            lhs = work[rows, pl.ds(j * EDGE, EDGE)]
            cut = p[:, (j - i - 1) * EDGE :]
            span = pl.ds(j * EDGE, total - j * EDGE)
            target = pl.ds(j * EDGE, EDGE)
            work[target, span] = work[target, span] - fine(lhs, cut, (((0,), (0,)), ((), ())))
    found = [None] * parts
    for i in reversed(range(parts)):
        x = made[i][:, (parts - i - 1) * EDGE :]
        for j in range(i + 1, parts):
            x = x - fine(made[i][:, (j - i - 1) * EDGE : (j - i) * EDGE], found[j])
        found[i] = x
    response = 0.0
    for i in range(parts):
        steer = steer_ref[pl.ds(i * EDGE, EDGE), :].astype(jnp.float32)
        response = response + jnp.sum(steer * found[i], axis=0, keepdims=True)
    for i in range(parts):
        out_ref[pl.ds(i * EDGE, EDGE), :] = (found[i] / response).astype(out_ref.dtype)


def make_weights(count, own, other, steering):
    size, beams = steering.shape
    vmem = pl.BlockSpec(memory_space=pltpu.VMEM)
    return pl.pallas_call(
        solve_kernel,
        out_shape=jax.ShapeDtypeStruct((size, beams), jnp.bfloat16),
        in_specs=[pl.BlockSpec(memory_space=pltpu.SMEM), vmem, vmem, vmem],
        out_specs=vmem,
        scratch_shapes=[pltpu.VMEM((size, size + beams), jnp.float32)],
        compiler_params=pltpu.CompilerParams(vmem_limit_bytes=16 * 1024 * 1024),
        cost_estimate=pl.CostEstimate(flops=10**9, bytes_accessed=2 * 10**6, transcendentals=0),
    )(count, own, other, steering)


def split_kernel(which_ref, x_ref, out_ref):
    out_ref[:, 0] = x_ref[0]


def split(x, which):
    halves, count, rows, wide = x.shape
    chunk = count // 4
    return pl.pallas_call(
        split_kernel,
        out_shape=jax.ShapeDtypeStruct((count, halves, rows, wide), x.dtype),
        grid_spec=pltpu.PrefetchScalarGridSpec(
            num_scalar_prefetch=1,
            grid=(halves, 4),
            in_specs=[pl.BlockSpec((1, chunk, rows, wide), lambda s, i, which: (which[s], i, 0, 0))],
            out_specs=pl.BlockSpec((chunk, 1, rows, wide), lambda s, i, which: (i, s, 0, 0)),
        ),
        compiler_params=pltpu.CompilerParams(vmem_limit_bytes=16 * 1024 * 1024),
        cost_estimate=pl.CostEstimate(flops=0, bytes_accessed=2 * x.size, transcendentals=0),
    )(which, x)


def body(halves, snapshots, steering, train_list, train_count):
    bin_total, gate_rows, channels = snapshots.shape
    half = lax.axis_index("half")
    group = bin_total // halves
    peers = [(0, 1), (1, 0)]
    which = jnp.stack([half, 1 - half]).astype(jnp.int32)
    base = (half * group).astype(jnp.int32)[None]

    def exchange(x):
        return lax.all_to_all(x, INNER, split_axis=0, concat_axis=0, tiled=True)

    other_list = lax.ppermute(train_list, "half", peers)
    other_count = lax.ppermute(train_count, "half", peers)
    outgoing = split(snapshots.reshape(halves, group, gate_rows, channels), which)
    outgoing, other_list, other_count, base, which = lax.optimization_barrier(
        (outgoing, other_list, other_count, base, which)
    )
    blocks = exchange(outgoing)

    other_gram = partial_gram(base, other_list, other_count, blocks, 1)
    arrived = lax.ppermute(other_gram, "half", peers)
    own_gram = partial_gram(base, train_list, train_count, blocks, 0)
    weights = make_weights(train_count, own_gram, arrived, steering[0])
    other_weights = lax.ppermute(weights, "half", peers)

    def beams(x, w):
        made = jnp.einsum("ngd,de->nge", x, w, preferred_element_type=jnp.float32)
        return made.astype(jnp.bfloat16)

    made = jnp.stack([beams(blocks[:, 0], weights), beams(blocks[:, 1], other_weights)], axis=1)
    made, here, there = lax.optimization_barrier((made, half, 1 - half))
    out = jnp.moveaxis(exchange(made), 1, 0)
    sets = [
        lax.dynamic_index_in_dim(out, at, 0, keepdims=False, allow_negative_indices=False)
        for at in (here, there)
    ]
    return jnp.concatenate(sets, axis=0)


def solution(mesh):
    ranges, dopplers = mesh.devices.shape
    halves = 2
    cut = Mesh(
        mesh.devices.reshape(halves, ranges // halves, dopplers), ("half", "inner", "doppler")
    )
    every = ("half", "inner", "doppler")

    def run(*args):
        return body(halves, *args)

    return jax.shard_map(
        run,
        mesh=cut,
        in_specs=(P(None, every, None), P(every, None, None), P(every, None), P(every)),
        out_specs=P(None, every, None),
        check_vma=False,
    )
```

```python
import jax
import jax.numpy as jnp
from jax import lax
from jax.experimental import pallas as pl
from jax.experimental.pallas import tpu as pltpu
from jax.sharding import Mesh
from jax.sharding import PartitionSpec as P

BLOCK = 128
LOADING = 0.1
EDGE = 128
STEP = 16
PACKED = 4 * EDGE + EDGE // 2 + 8
INNER = ("inner", "doppler")
EVERY = ("half",) + INNER
VMEM_BYTES = 16 * 1024 * 1024
SPLIT_BYTES = 16 * 1024 * 1024


def edge_iota(dim, rows=EDGE):
    return lax.broadcasted_iota(jnp.int32, (rows, EDGE), dim)


def gram_kernel(base_ref, list_ref, count_ref, blocks_ref, out_ref, chosen):
    group, _, rows, size = blocks_ref.shape
    for p in range(list_ref.shape[1]):
        chosen[list_ref[0, p]] = (p < count_ref[0]).astype(jnp.int32)
    every = [blocks_ref[n, 0] for n in range(group)]
    kept = [
        jnp.where(chosen[base_ref[0] + n] > 0, x, jnp.zeros_like(x)) for n, x in enumerate(every)
    ]
    every = jnp.concatenate(every, axis=0)
    kept = jnp.concatenate(kept, axis=0)

    def strip(i):
        return lax.dot_general(
            kept[:, i * EDGE : (i + 1) * EDGE], every[:, i * EDGE :], (((0,), (0,)), ((), ())),
            preferred_element_type=jnp.float32,
        )

    half = EDGE // 2
    r, c = edge_iota(0), edge_iota(1)
    zero, one, two = strip(0), strip(1), strip(2)
    out_ref[pl.ds(0, EDGE), :] = zero[:, EDGE : 2 * EDGE]
    out_ref[pl.ds(EDGE, EDGE), :] = zero[:, 2 * EDGE :]
    out_ref[pl.ds(2 * EDGE, EDGE), :] = one[:, EDGE:]
    out_ref[pl.ds(3 * EDGE, EDGE), :] = jnp.where(r <= c, zero[:, :EDGE], one[:, :EDGE])
    low = pltpu.roll(two[half:], half, axis=1)
    rh, ch = r[:half], c[:half]
    out_ref[pl.ds(4 * EDGE, half), :] = jnp.where((ch < half) & (rh > ch), low, two[:half])
    first = jnp.sum(jnp.where(r == c, one[:, :EDGE], 0.0), axis=0, keepdims=True)
    second = jnp.sum(jnp.where(rh == ch, low, 0.0), axis=0, keepdims=True)
    s = edge_iota(0, 8)
    out_ref[pl.ds(4 * EDGE + half, 8), :] = jnp.where(s == 0, first, jnp.where(s == 1, second, 0.0))


def partial_gram(which, base, lists, counts, blocks):
    group, _, rows, size = blocks.shape
    smem = pl.BlockSpec(memory_space=pltpu.SMEM)
    return pl.pallas_call(
        gram_kernel,
        out_shape=jax.ShapeDtypeStruct((PACKED, EDGE), jnp.float32),
        grid=(1,),
        in_specs=[
            smem, smem, smem, pl.BlockSpec((group, 1, rows, size), lambda i: (0, which, 0, 0))
        ],
        out_specs=pl.BlockSpec((PACKED, EDGE), lambda i: (0, 0)),
        scratch_shapes=[pltpu.SMEM((lists.shape[1],), jnp.int32)],
        compiler_params=pltpu.CompilerParams(vmem_limit_bytes=2 * VMEM_BYTES),
        cost_estimate=pl.CostEstimate(
            flops=2 * group * rows * size * size,
            bytes_accessed=2 * group * rows * size,
            transcendentals=0,
        ),
    )(base, lists, counts, blocks)


def unpack(packed):
    half = EDGE // 2
    r, c = edge_iota(0), edge_iota(1)
    both = packed[3 * EDGE : 4 * EDGE]
    turned = both.T
    diag = packed[4 * EDGE + half : 4 * EDGE + half + 8]
    zero = jnp.where(r <= c, both, turned)
    one = jnp.where(r > c, both, jnp.where(r < c, turned, diag[0:1]))
    top = packed[4 * EDGE : 4 * EDGE + half]
    side = jnp.concatenate([top, jnp.zeros_like(top)], axis=0).T
    rh, ch = r[:half], c[:half]
    upper = jnp.where((ch < half) & (rh > ch), side[:half], top)
    low = jnp.where(
        rh > ch,
        top,
        jnp.where(rh < ch, side[:half], diag[1:2]),
    )
    lower = jnp.where(ch < half, side[half:], pltpu.roll(low, half, axis=1))
    two = jnp.concatenate([upper, lower], axis=0)
    return [
        jnp.concatenate([zero, packed[:EDGE], packed[EDGE : 2 * EDGE]], axis=1),
        jnp.concatenate([one, packed[2 * EDGE : 3 * EDGE]], axis=1),
        two,
    ]


def fine(a, b, dims=(((1,), (0,)), ((), ()))):
    return lax.dot_general(
        a, b, dims, precision=lax.Precision.HIGHEST, preferred_element_type=jnp.float32
    )


def thirds(x):
    hi = x.astype(jnp.bfloat16)
    rest = x - hi.astype(jnp.float32)
    mid = rest.astype(jnp.bfloat16)
    low = (rest - mid.astype(jnp.float32)).astype(jnp.bfloat16)
    return hi, mid, low


def outer(a, b):
    ah, am, al = thirds(a)
    bh, bm, bl = thirds(b)
    left = jnp.concatenate([ah, ah, ah, am, am, al], axis=0)
    right = jnp.concatenate([bh, bm, bl, bh, bm, bh], axis=0)
    return lax.dot_general(
        left, right, (((0,), (0,)), ((), ())), preferred_element_type=jnp.float32
    )


def eliminate(rows, cols):
    full = (STEP, EDGE)
    sub = lax.broadcasted_iota(jnp.int32, full, 0)

    def row(x, k):
        return jnp.broadcast_to(x[k : k + 1], full)

    cols = list(cols)
    for k in range(0, STEP, 2):
        one, two = sub == k, sub == k + 1
        here = one | two
        a, b, c = row(cols[k], k), row(cols[k + 1], k), row(cols[k + 1], k + 1)
        inv = 1.0 / (a * c - b * b)
        first = jnp.where(one, 1.0, jnp.where(two, 0.0, -cols[k]))
        second = jnp.where(two, 1.0, jnp.where(one, 0.0, -cols[k + 1]))

        def step(x):
            r, s = row(x, k), row(x, k + 1)
            up = (c * r - b * s) * inv
            down = (a * s - b * r) * inv
            return (jnp.where(here, 0.0, x) + first * up) + second * down

        for i in range(k + 2, STEP):
            cols[i] = step(cols[i])
        rows = step(rows)
    return rows


def negative_inverse(strips):
    full = (STEP, EDGE)
    panels = EDGE // STEP
    sub = lax.broadcasted_iota(jnp.int32, full, 0)
    lane = lax.broadcasted_iota(jnp.int32, full, 1)

    def spread(x, at):
        return [jnp.broadcast_to(x[:, at + i : at + i + 1], full) for i in range(STEP)]

    rows = strips[0]
    for p in range(panels):
        at = p * STEP
        inside = (lane >= at) & (lane < at + STEP)
        swept = jnp.where(inside, jnp.where(lane == sub + at, -1.0, 0.0), rows)
        weights = spread(strips[p + 1], at) if p + 1 < panels else None
        solved = eliminate(swept, spread(rows, at))
        if weights is not None:
            terms = [w * jnp.broadcast_to(solved[k : k + 1], full) for k, w in enumerate(weights)]
            while len(terms) > 1:
                terms = [x + y for x, y in zip(terms[::2], terms[1::2])]
            rows = jnp.where(inside, 0.0, strips[p + 1]) - terms[0]
        change = outer(swept, solved)
        strips = [
            rows
            if q == p + 1
            else (jnp.zeros(full, jnp.float32) if q == p else jnp.where(inside, 0.0, strips[q]))
            - change[q * STEP : (q + 1) * STEP]
            for q in range(panels)
        ]
    return jnp.concatenate(strips, axis=0)


def solve_kernel(count_ref, own_ref, other_ref, steer_ref, out_ref, work):
    size = steer_ref.shape[0]
    parts = size // EDGE
    inv_scale = 1.0 / (BLOCK * count_ref[0]).astype(jnp.float32)
    strips = unpack(own_ref[...] + other_ref[...])
    for i in range(parts):
        width = size - i * EDGE
        rows = pl.ds(i * EDGE, EDGE)
        r = lax.broadcasted_iota(jnp.int32, (EDGE, width), 0)
        c = lax.broadcasted_iota(jnp.int32, (EDGE, width), 1)
        work[rows, pl.ds(i * EDGE, width)] = strips[i] * inv_scale + jnp.where(r == c, LOADING, 0.0)
    beams = steer_ref.shape[1]
    work[:, pl.ds(size, beams)] = steer_ref[...].astype(jnp.float32)
    total = size + beams
    made = []
    for i in range(parts):
        rows = pl.ds(i * EDGE, EDGE)
        strips = [
            work[pl.ds(i * EDGE + q * STEP, STEP), pl.ds(i * EDGE, EDGE)]
            for q in range(EDGE // STEP)
        ]
        minus = negative_inverse(strips)
        right = work[rows, pl.ds((i + 1) * EDGE, total - (i + 1) * EDGE)]
        p = -fine(minus, right)
        made.append(p)
        for j in range(i + 1, parts):
            lhs = work[rows, pl.ds(j * EDGE, EDGE)]
            cut = p[:, (j - i - 1) * EDGE :]
            span = pl.ds(j * EDGE, total - j * EDGE)
            target = pl.ds(j * EDGE, EDGE)
            work[target, span] = work[target, span] - fine(lhs, cut, (((0,), (0,)), ((), ())))
    found = [None] * parts
    for i in reversed(range(parts)):
        x = made[i][:, (parts - i - 1) * EDGE :]
        for j in range(i + 1, parts):
            x = x - fine(made[i][:, (j - i - 1) * EDGE : (j - i) * EDGE], found[j])
        found[i] = x
    response = 0.0
    for i in range(parts):
        steer = steer_ref[pl.ds(i * EDGE, EDGE), :].astype(jnp.float32)
        response = response + jnp.sum(steer * found[i], axis=0, keepdims=True)
    for i in range(parts):
        out_ref[pl.ds(i * EDGE, EDGE), :] = (found[i] / response).astype(out_ref.dtype)


def make_weights(count, own, other, steering):
    size, beams = steering.shape
    vmem = pl.BlockSpec(memory_space=pltpu.VMEM)
    return pl.pallas_call(
        solve_kernel,
        out_shape=jax.ShapeDtypeStruct((size, beams), jnp.bfloat16),
        in_specs=[pl.BlockSpec(memory_space=pltpu.SMEM), vmem, vmem, vmem],
        out_specs=vmem,
        scratch_shapes=[pltpu.VMEM((size, size + beams), jnp.float32)],
        compiler_params=pltpu.CompilerParams(vmem_limit_bytes=VMEM_BYTES),
        cost_estimate=pl.CostEstimate(flops=10**9, bytes_accessed=2 * 10**6, transcendentals=0),
    )(count, own, other, steering)


def split_kernel(which_ref, x_ref, out_ref):
    out_ref[:, 0] = x_ref[0]


def split(which, x):
    halves, group, rows, wide = x.shape
    chunks = 4
    return pl.pallas_call(
        split_kernel,
        out_shape=jax.ShapeDtypeStruct((group, halves, rows, wide), x.dtype),
        grid_spec=pltpu.PrefetchScalarGridSpec(
            num_scalar_prefetch=1,
            grid=(halves, chunks),
            in_specs=[
                pl.BlockSpec(
                    (1, group // chunks, rows, wide), lambda s, i, which: (which[s], i, 0, 0)
                )
            ],
            out_specs=pl.BlockSpec(
                (group // chunks, 1, rows, wide), lambda s, i, which: (i, s, 0, 0)
            ),
        ),
        compiler_params=pltpu.CompilerParams(vmem_limit_bytes=SPLIT_BYTES),
        cost_estimate=pl.CostEstimate(flops=0, bytes_accessed=2 * x.size, transcendentals=0),
    )(which, x)


def body(halves, snapshots, steering, train_list, train_count):
    bin_total, gate_rows, channels = snapshots.shape
    half = lax.axis_index("half").astype(jnp.int32)
    group = bin_total // halves
    order, base = jnp.stack([half, 1 - half]), half[None] * group
    peers = [(0, 1), (1, 0)]

    def exchange(x):
        return lax.all_to_all(x, INNER, split_axis=0, concat_axis=0, tiled=True)

    other_list = lax.ppermute(train_list, "half", peers)
    other_count = lax.ppermute(train_count, "half", peers)
    outgoing = split(order, snapshots.reshape(halves, group, gate_rows, channels))
    outgoing, other_list, other_count, base = lax.optimization_barrier(
        (outgoing, other_list, other_count, base)
    )
    blocks = exchange(outgoing)

    other_gram = partial_gram(1, base, other_list, other_count, blocks)
    arrived = lax.ppermute(other_gram, "half", peers)
    own_gram = partial_gram(0, base, train_list, train_count, blocks)
    weights = make_weights(train_count, own_gram, arrived, steering[0])
    other_weights = lax.ppermute(weights, "half", peers)

    def beams(x, w):
        made = jnp.einsum("ngd,de->nge", x, w, preferred_element_type=jnp.float32)
        return made.astype(jnp.bfloat16)

    made = jnp.stack([beams(blocks[:, 0], weights), beams(blocks[:, 1], other_weights)], axis=1)
    made, here, there = lax.optimization_barrier((made, half, 1 - half))
    out = jnp.moveaxis(exchange(made), 1, 0)
    sets = [
        lax.dynamic_index_in_dim(out, at, 0, keepdims=False, allow_negative_indices=False)
        for at in (here, there)
    ]
    return jnp.concatenate(sets, axis=0)


def solution(mesh):
    ranges, dopplers = mesh.devices.shape
    halves = 2
    cut = Mesh(mesh.devices.reshape(halves, ranges // halves, dopplers), EVERY)

    def run(*args):
        return body(halves, *args)

    return jax.shard_map(
        run,
        mesh=cut,
        in_specs=(P(None, EVERY, None), P(EVERY, None, None), P(EVERY, None), P(EVERY)),
        out_specs=P(None, EVERY, None),
        check_vma=False,
    )
```

```python
import functools

import jax
import jax.numpy as jnp
from jax import lax
from jax.experimental import pallas as pl
from jax.experimental.pallas import tpu as pltpu
from jax.sharding import Mesh
from jax.sharding import PartitionSpec as P

BLOCK = 128
LOADING = 0.1
EDGE = 128
STEP = 16
PACKED = 4 * EDGE + EDGE // 2 + 8
INNER = ("inner", "doppler")
EVERY = ("half",) + INNER
VMEM_BYTES = 16 * 1024 * 1024
SPLIT_BYTES = 16 * 1024 * 1024


def edge_iota(dim, rows=EDGE):
    return lax.broadcasted_iota(jnp.int32, (rows, EDGE), dim)


def gram_kernel(which, base_ref, list_ref, count_ref, blocks_ref, out_ref, chosen):
    group, _, rows, size = blocks_ref.shape
    for p in range(list_ref.shape[1]):
        chosen[list_ref[0, p]] = (p < count_ref[0]).astype(jnp.int32)
    every = [blocks_ref[n, which] for n in range(group)]
    kept = [
        jnp.where(chosen[base_ref[0] + n] > 0, x, jnp.zeros_like(x)) for n, x in enumerate(every)
    ]
    every = jnp.concatenate(every, axis=0)
    kept = jnp.concatenate(kept, axis=0)

    def strip(i):
        return lax.dot_general(
            kept[:, i * EDGE : (i + 1) * EDGE], every[:, i * EDGE :], (((0,), (0,)), ((), ())),
            preferred_element_type=jnp.float32,
        )

    half = EDGE // 2
    r, c = edge_iota(0), edge_iota(1)
    zero, one, two = strip(0), strip(1), strip(2)
    out_ref[pl.ds(0, EDGE), :] = zero[:, EDGE : 2 * EDGE]
    out_ref[pl.ds(EDGE, EDGE), :] = zero[:, 2 * EDGE :]
    out_ref[pl.ds(2 * EDGE, EDGE), :] = one[:, EDGE:]
    out_ref[pl.ds(3 * EDGE, EDGE), :] = jnp.where(r <= c, zero[:, :EDGE], one[:, :EDGE])
    low = pltpu.roll(two[half:], half, axis=1)
    rh, ch = r[:half], c[:half]
    out_ref[pl.ds(4 * EDGE, half), :] = jnp.where((ch < half) & (rh > ch), low, two[:half])
    first = jnp.sum(jnp.where(r == c, one[:, :EDGE], 0.0), axis=0, keepdims=True)
    second = jnp.sum(jnp.where(rh == ch, low, 0.0), axis=0, keepdims=True)
    s = edge_iota(0, 8)
    out_ref[pl.ds(4 * EDGE + half, 8), :] = jnp.where(s == 0, first, jnp.where(s == 1, second, 0.0))


def partial_gram(which, base, lists, counts, blocks):
    group, _, rows, size = blocks.shape
    smem = pl.BlockSpec(memory_space=pltpu.SMEM)
    vmem = pl.BlockSpec(memory_space=pltpu.VMEM)
    return pl.pallas_call(
        functools.partial(gram_kernel, which),
        out_shape=jax.ShapeDtypeStruct((PACKED, EDGE), jnp.float32),
        in_specs=[smem, smem, smem, vmem],
        out_specs=vmem,
        scratch_shapes=[pltpu.SMEM((lists.shape[1],), jnp.int32)],
        compiler_params=pltpu.CompilerParams(vmem_limit_bytes=3 * VMEM_BYTES),
        cost_estimate=pl.CostEstimate(
            flops=2 * group * rows * size * size,
            bytes_accessed=2 * group * rows * size,
            transcendentals=0,
        ),
    )(base, lists, counts, blocks)


def unpack(packed):
    half = EDGE // 2
    r, c = edge_iota(0), edge_iota(1)
    both = packed[3 * EDGE : 4 * EDGE]
    turned = both.T
    diag = packed[4 * EDGE + half : 4 * EDGE + half + 8]
    zero = jnp.where(r <= c, both, turned)
    one = jnp.where(r > c, both, jnp.where(r < c, turned, diag[0:1]))
    top = packed[4 * EDGE : 4 * EDGE + half]
    side = jnp.concatenate([top, jnp.zeros_like(top)], axis=0).T
    rh, ch = r[:half], c[:half]
    upper = jnp.where((ch < half) & (rh > ch), side[:half], top)
    low = jnp.where(
        rh > ch,
        top,
        jnp.where(rh < ch, side[:half], diag[1:2]),
    )
    lower = jnp.where(ch < half, side[half:], pltpu.roll(low, half, axis=1))
    two = jnp.concatenate([upper, lower], axis=0)
    return [
        jnp.concatenate([zero, packed[:EDGE], packed[EDGE : 2 * EDGE]], axis=1),
        jnp.concatenate([one, packed[2 * EDGE : 3 * EDGE]], axis=1),
        two,
    ]


def fine(a, b, dims=(((1,), (0,)), ((), ()))):
    return lax.dot_general(
        a, b, dims, precision=lax.Precision.HIGHEST, preferred_element_type=jnp.float32
    )


def thirds(x):
    hi = x.astype(jnp.bfloat16)
    rest = x - hi.astype(jnp.float32)
    mid = rest.astype(jnp.bfloat16)
    low = (rest - mid.astype(jnp.float32)).astype(jnp.bfloat16)
    return hi, mid, low


def outer(a, b):
    ah, am, al = thirds(a)
    bh, bm, bl = thirds(b)
    left = jnp.concatenate([ah, ah, ah, am, am, al], axis=0)
    right = jnp.concatenate([bh, bm, bl, bh, bm, bh], axis=0)
    return lax.dot_general(
        left, right, (((0,), (0,)), ((), ())), preferred_element_type=jnp.float32
    )


def eliminate(rows, cols):
    full = (STEP, EDGE)
    sub = lax.broadcasted_iota(jnp.int32, full, 0)

    def row(x, k):
        return jnp.broadcast_to(x[k : k + 1], full)

    cols = list(cols)
    for k in range(0, STEP, 2):
        one, two = sub == k, sub == k + 1
        here = one | two
        a, b, c = row(cols[k], k), row(cols[k + 1], k), row(cols[k + 1], k + 1)
        inv = 1.0 / (a * c - b * b)
        first = jnp.where(one, 1.0, jnp.where(two, 0.0, -cols[k]))
        second = jnp.where(two, 1.0, jnp.where(one, 0.0, -cols[k + 1]))

        left = (first * c - second * b) * inv
        after = (second * a - first * b) * inv

        def step(x):
            r, s = row(x, k), row(x, k + 1)
            return jnp.where(here, 0.0, x) + (left * r + after * s)

        for i in range(k + 2, STEP):
            cols[i] = step(cols[i])
        rows = step(rows)
    return rows


def negative_inverse(strips):
    full = (STEP, EDGE)
    panels = EDGE // STEP
    sub = lax.broadcasted_iota(jnp.int32, full, 0)
    lane = lax.broadcasted_iota(jnp.int32, full, 1)

    def spread(x, at):
        return [
            jnp.take_along_axis(
                x, jnp.full(full, at + i, jnp.int32), axis=1, mode="promise_in_bounds"
            )
            for i in range(STEP)
        ]

    rows = strips[0]
    for p in range(panels):
        at = p * STEP
        inside = (lane >= at) & (lane < at + STEP)
        swept = jnp.where(inside, jnp.where(lane == sub + at, -1.0, 0.0), rows)
        weights = spread(strips[p + 1], at) if p + 1 < panels else None
        solved = eliminate(swept, spread(rows, at))
        if weights is not None:
            terms = [w * jnp.broadcast_to(solved[k : k + 1], full) for k, w in enumerate(weights)]
            while len(terms) > 1:
                terms = [x + y for x, y in zip(terms[::2], terms[1::2])]
            rows = jnp.where(inside, 0.0, strips[p + 1]) - terms[0]
        change = outer(swept, solved)
        strips = [
            rows
            if q == p + 1
            else (jnp.zeros(full, jnp.float32) if q == p else jnp.where(inside, 0.0, strips[q]))
            - change[q * STEP : (q + 1) * STEP]
            for q in range(panels)
        ]
    return jnp.concatenate(strips, axis=0)


def solve_kernel(count_ref, own_ref, other_ref, steer_ref, out_ref):
    size, beams = steer_ref.shape
    parts = size // EDGE
    inv_scale = 1.0 / (BLOCK * count_ref[0]).astype(jnp.float32)
    strips = unpack(own_ref[...] + other_ref[...])
    loading = jnp.where(edge_iota(0) == edge_iota(1), LOADING, 0.0)
    rest = []
    for i in range(parts):
        row = [strips[i][:, j * EDGE : (j + 1) * EDGE] * inv_scale for j in range(parts - i)]
        row[0] = row[0] + loading
        rest.append(row)
    right = [steer_ref[pl.ds(i * EDGE, EDGE), :].astype(jnp.float32) for i in range(parts)]
    turned = (((0,), (0,)), ((), ()))
    made = []
    for i in range(parts):
        diag = rest[i][0]
        minus = negative_inverse([diag[q : q + STEP] for q in range(0, EDGE, STEP)])
        lhs = rest[i][1:]
        plus = [None] * len(lhs)
        for j in range(len(lhs)):
            plus[j] = -fine(minus, lhs[j])
            if j == 0:
                rest[i + 1][0] = rest[i + 1][0] - fine(lhs[0], plus[0], turned)
        last = -fine(minus, right[i])
        for j in range(len(lhs)):
            for k in range(j, len(lhs)):
                if k > 0:
                    rest[i + 1 + j][k - j] = rest[i + 1 + j][k - j] - fine(lhs[j], plus[k], turned)
            right[i + 1 + j] = right[i + 1 + j] - fine(lhs[j], last, turned)
        made.append((plus, last))
    found = [None] * parts
    for i in reversed(range(parts)):
        plus, x = made[i]
        for j, p in enumerate(plus):
            x = x - fine(p, found[i + 1 + j])
        found[i] = x
    response = 0.0
    for i in range(parts):
        steer = steer_ref[pl.ds(i * EDGE, EDGE), :].astype(jnp.float32)
        response = response + jnp.sum(steer * found[i], axis=0, keepdims=True)
    for i in range(parts):
        out_ref[pl.ds(i * EDGE, EDGE), :] = (found[i] / response).astype(out_ref.dtype)


def make_weights(count, own, other, steering):
    size, beams = steering.shape
    vmem = pl.BlockSpec(memory_space=pltpu.VMEM)
    return pl.pallas_call(
        solve_kernel,
        out_shape=jax.ShapeDtypeStruct((size, beams), jnp.bfloat16),
        in_specs=[pl.BlockSpec(memory_space=pltpu.SMEM), vmem, vmem, vmem],
        out_specs=vmem,
        compiler_params=pltpu.CompilerParams(vmem_limit_bytes=VMEM_BYTES),
        cost_estimate=pl.CostEstimate(flops=10**9, bytes_accessed=2 * 10**6, transcendentals=0),
    )(count, own, other, steering)


def split_kernel(which_ref, x_ref, out_ref):
    out_ref[:, 0] = x_ref[0]


def split(which, x):
    halves, group, rows, wide = x.shape
    chunks = 4
    return pl.pallas_call(
        split_kernel,
        out_shape=jax.ShapeDtypeStruct((group, halves, rows, wide), x.dtype),
        grid_spec=pltpu.PrefetchScalarGridSpec(
            num_scalar_prefetch=1,
            grid=(halves, chunks),
            in_specs=[
                pl.BlockSpec(
                    (1, group // chunks, rows, wide), lambda s, i, which: (which[s], i, 0, 0)
                )
            ],
            out_specs=pl.BlockSpec(
                (group // chunks, 1, rows, wide), lambda s, i, which: (i, s, 0, 0)
            ),
        ),
        compiler_params=pltpu.CompilerParams(vmem_limit_bytes=SPLIT_BYTES),
        cost_estimate=pl.CostEstimate(flops=0, bytes_accessed=2 * x.size, transcendentals=0),
    )(which, x)


def body(halves, snapshots, steering, train_list, train_count):
    bin_total, gate_rows, channels = snapshots.shape
    half = lax.axis_index("half").astype(jnp.int32)
    group = bin_total // halves
    order, base = jnp.stack([half, 1 - half]), half[None] * group
    peers = [(0, 1), (1, 0)]

    def exchange(x):
        return lax.all_to_all(x, INNER, split_axis=0, concat_axis=0, tiled=True)

    other_list = lax.ppermute(train_list, "half", peers)
    other_count = lax.ppermute(train_count, "half", peers)
    outgoing = split(order, snapshots.reshape(halves, group, gate_rows, channels))
    outgoing, other_list, other_count, base = lax.optimization_barrier(
        (outgoing, other_list, other_count, base)
    )
    blocks = exchange(outgoing)

    other_gram = partial_gram(1, base, other_list, other_count, blocks)
    arrived = lax.ppermute(other_gram, "half", peers)
    own_gram = partial_gram(0, base, train_list, train_count, blocks)
    weights = make_weights(train_count, own_gram, arrived, steering[0])
    other_weights = lax.ppermute(weights, "half", peers)

    def beams(x, w):
        made = jnp.einsum("ngd,de->nge", x, w, preferred_element_type=jnp.float32)
        return made.astype(jnp.bfloat16)

    made = jnp.stack([beams(blocks[:, 0], weights), beams(blocks[:, 1], other_weights)], axis=1)
    made, here, there = lax.optimization_barrier((made, half, 1 - half))
    out = jnp.moveaxis(exchange(made), 1, 0)
    sets = [
        lax.dynamic_index_in_dim(out, at, 0, keepdims=False, allow_negative_indices=False)
        for at in (here, there)
    ]
    return jnp.concatenate(sets, axis=0)


def solution(mesh):
    ranges, dopplers = mesh.devices.shape
    halves = 2
    cut = Mesh(mesh.devices.reshape(halves, ranges // halves, dopplers), EVERY)

    def run(*args):
        return body(halves, *args)

    return jax.shard_map(
        run,
        mesh=cut,
        in_specs=(P(None, EVERY, None), P(EVERY, None, None), P(EVERY, None), P(EVERY)),
        out_specs=P(None, EVERY, None),
        check_vma=False,
    )
```

```python
import functools

import jax
import jax.numpy as jnp
from jax import lax
from jax.experimental import pallas as pl
from jax.experimental.pallas import tpu as pltpu
from jax.sharding import Mesh
from jax.sharding import PartitionSpec as P

BLOCK = 128
LOADING = 0.1
EDGE = 128
STEP = 16
PACKED = (EDGE, 2 * EDGE, EDGE + EDGE // 2 + 8)
INNER = ("inner", "doppler")
EVERY = ("half",) + INNER
VMEM_BYTES = 16 * 1024 * 1024
SPLIT_BYTES = 16 * 1024 * 1024


def edge_iota(dim, rows=EDGE):
    return lax.broadcasted_iota(jnp.int32, (rows, EDGE), dim)


def gram_kernel(which, base_ref, list_ref, count_ref, blocks_ref, corner_ref, side_ref, late_ref, chosen):
    group, _, rows, size = blocks_ref.shape
    for p in range(list_ref.shape[1]):
        chosen[list_ref[0, p]] = (p < count_ref[0]).astype(jnp.int32)
    every = [blocks_ref[n, which] for n in range(group)]
    kept = [
        jnp.where(chosen[base_ref[0] + n] > 0, x, jnp.zeros_like(x)) for n, x in enumerate(every)
    ]
    every = jnp.concatenate(every, axis=0)
    kept = jnp.concatenate(kept, axis=0)

    def strip(i):
        return lax.dot_general(
            kept[:, i * EDGE : (i + 1) * EDGE], every[:, i * EDGE :], (((0,), (0,)), ((), ())),
            preferred_element_type=jnp.float32,
        )

    half = EDGE // 2
    r, c = edge_iota(0), edge_iota(1)
    zero, one, two = strip(0), strip(1), strip(2)
    corner_ref[...] = jnp.where(r <= c, zero[:, :EDGE], one[:, :EDGE])
    side_ref[pl.ds(0, EDGE), :] = zero[:, EDGE : 2 * EDGE]
    side_ref[pl.ds(EDGE, EDGE), :] = zero[:, 2 * EDGE :]
    late_ref[pl.ds(0, EDGE), :] = one[:, EDGE:]
    low = pltpu.roll(two[half:], half, axis=1)
    rh, ch = r[:half], c[:half]
    late_ref[pl.ds(EDGE, half), :] = jnp.where((ch < half) & (rh > ch), low, two[:half])
    first = jnp.sum(jnp.where(r == c, one[:, :EDGE], 0.0), axis=0, keepdims=True)
    second = jnp.sum(jnp.where(rh == ch, low, 0.0), axis=0, keepdims=True)
    s = edge_iota(0, 8)
    late_ref[pl.ds(EDGE + half, 8), :] = jnp.where(s == 0, first, jnp.where(s == 1, second, 0.0))


def partial_gram(which, base, lists, counts, blocks):
    group, _, rows, size = blocks.shape
    smem = pl.BlockSpec(memory_space=pltpu.SMEM)
    vmem = pl.BlockSpec(memory_space=pltpu.VMEM)
    return pl.pallas_call(
        functools.partial(gram_kernel, which),
        out_shape=[jax.ShapeDtypeStruct((n, EDGE), jnp.float32) for n in PACKED],
        in_specs=[smem, smem, smem, vmem],
        out_specs=[vmem] * len(PACKED),
        scratch_shapes=[pltpu.SMEM((lists.shape[1],), jnp.int32)],
        compiler_params=pltpu.CompilerParams(vmem_limit_bytes=3 * VMEM_BYTES),
        cost_estimate=pl.CostEstimate(
            flops=2 * group * rows * size * size,
            bytes_accessed=2 * group * rows * size,
            transcendentals=0,
        ),
    )(base, lists, counts, blocks)


def unpack_late(both, late):
    half = EDGE // 2
    r, c = edge_iota(0), edge_iota(1)
    diag = late[EDGE + half :]
    one = jnp.where(r > c, both, jnp.where(r < c, both.T, diag[0:1]))
    top = late[EDGE : EDGE + half]
    side = jnp.concatenate([top, jnp.zeros_like(top)], axis=0).T
    rh, ch = r[:half], c[:half]
    upper = jnp.where((ch < half) & (rh > ch), side[:half], top)
    low = jnp.where(rh > ch, top, jnp.where(rh < ch, side[:half], diag[1:2]))
    lower = jnp.where(ch < half, side[half:], pltpu.roll(low, half, axis=1))
    return [one, late[:EDGE]], [jnp.concatenate([upper, lower], axis=0)]


def fine(a, b, dims=(((1,), (0,)), ((), ()))):
    return lax.dot_general(
        a, b, dims, precision=lax.Precision.HIGHEST, preferred_element_type=jnp.float32
    )


def thirds(x):
    hi = x.astype(jnp.bfloat16)
    rest = x - hi.astype(jnp.float32)
    mid = rest.astype(jnp.bfloat16)
    low = (rest - mid.astype(jnp.float32)).astype(jnp.bfloat16)
    return hi, mid, low


def outer(a, b):
    ah, am, al = thirds(a)
    bh, bm, bl = thirds(b)
    left = jnp.concatenate([ah, ah, ah, am, am, al], axis=0)
    right = jnp.concatenate([bh, bm, bl, bh, bm, bh], axis=0)
    return lax.dot_general(
        left, right, (((0,), (0,)), ((), ())), preferred_element_type=jnp.float32
    )


def eliminate(rows, cols):
    full = (STEP, EDGE)
    sub = lax.broadcasted_iota(jnp.int32, full, 0)

    def row(x, k):
        return jnp.broadcast_to(x[k : k + 1], full)

    cols = list(cols)
    for k in range(0, STEP, 2):
        one, two = sub == k, sub == k + 1
        here = one | two
        a, b, c = row(cols[k], k), row(cols[k + 1], k), row(cols[k + 1], k + 1)
        inv = 1.0 / (a * c - b * b)
        first = jnp.where(one, 1.0, jnp.where(two, 0.0, -cols[k]))
        second = jnp.where(two, 1.0, jnp.where(one, 0.0, -cols[k + 1]))

        left = (first * c - second * b) * inv
        after = (second * a - first * b) * inv

        def step(x):
            r, s = row(x, k), row(x, k + 1)
            return jnp.where(here, 0.0, x) + (left * r + after * s)

        for i in range(k + 2, STEP):
            cols[i] = step(cols[i])
        rows = step(rows)
    return rows


def negative_inverse(strips):
    full = (STEP, EDGE)
    panels = EDGE // STEP
    sub = lax.broadcasted_iota(jnp.int32, full, 0)
    lane = lax.broadcasted_iota(jnp.int32, full, 1)

    def spread(x, at):
        return [
            jnp.take_along_axis(
                x, jnp.full(full, at + i, jnp.int32), axis=1, mode="promise_in_bounds"
            )
            for i in range(STEP)
        ]

    rows = strips[0]
    for p in range(panels):
        at = p * STEP
        inside = (lane >= at) & (lane < at + STEP)
        swept = jnp.where(inside, jnp.where(lane == sub + at, -1.0, 0.0), rows)
        weights = spread(strips[p + 1], at) if p + 1 < panels else None
        solved = eliminate(swept, spread(rows, at))
        if weights is not None:
            terms = [w * jnp.broadcast_to(solved[k : k + 1], full) for k, w in enumerate(weights)]
            while len(terms) > 1:
                terms = [x + y for x, y in zip(terms[::2], terms[1::2])]
            rows = jnp.where(inside, 0.0, strips[p + 1]) - terms[0]
        change = outer(swept, solved)
        strips = [
            rows
            if q == p + 1
            else (jnp.zeros(full, jnp.float32) if q == p else jnp.where(inside, 0.0, strips[q]))
            - change[q * STEP : (q + 1) * STEP]
            for q in range(panels)
        ]
    return jnp.concatenate(strips, axis=0)


TURNED = (((0,), (0,)), ((), ()))


def covariance_blocks(row, count_ref):
    inv_scale = 1.0 / (BLOCK * count_ref[0]).astype(jnp.float32)
    row = [x * inv_scale for x in row]
    row[0] = row[0] + jnp.where(edge_iota(0) == edge_iota(1), LOADING, 0.0)
    return row


def minus_inverse(block):
    return negative_inverse([block[q : q + STEP] for q in range(0, EDGE, STEP)])


def corner_kernel(count_ref, own_ref, other_ref, minus_ref):
    both = own_ref[...] + other_ref[...]
    block = jnp.where(edge_iota(0) <= edge_iota(1), both, both.T)
    minus_ref[...] = minus_inverse(covariance_blocks([block], count_ref)[0])


def side_kernel(count_ref, own_ref, other_ref, steer_ref, minus_ref, made_ref, less_ref):
    inv_scale = 1.0 / (BLOCK * count_ref[0]).astype(jnp.float32)
    side = (own_ref[...] + other_ref[...]) * inv_scale
    near, far = side[:EDGE], side[EDGE:]
    right = steer_ref[pl.ds(0, EDGE), :].astype(jnp.float32)
    made = -fine(minus_ref[...], jnp.concatenate([near, far, right], axis=1))
    made_ref[...] = made
    less_ref[0] = fine(near, made, TURNED)
    less_ref[1] = fine(far, made, TURNED)


def late_kernel(
    count_ref, own_corner, other_corner, own_late, other_late, steer_ref, made_ref, less_ref, out_ref
):
    size = steer_ref.shape[0]
    strips = unpack_late(
        own_corner[...] + other_corner[...], own_late[...] + other_late[...]
    )
    one, two = [covariance_blocks(list(x), count_ref) for x in strips]
    one = [x - less_ref[0, :, pl.ds(i * EDGE, EDGE)] for i, x in enumerate(one)]
    right = [
        steer_ref[pl.ds(i * EDGE, EDGE), :].astype(jnp.float32) - less_ref[i - 1, :, 2 * EDGE :]
        for i in (1, 2)
    ]
    minus = minus_inverse(one[0])
    step = -fine(minus, one[1])
    left = two[0] - less_ref[1, :, pl.ds(EDGE, EDGE)] - fine(one[1], step, TURNED)
    middle = -fine(minus, right[0])
    last = right[1] - fine(one[1], middle, TURNED)
    found = [None, None, -fine(minus_inverse(left), last)]
    found[1] = middle - fine(step, found[2])
    made = made_ref[...]
    found[0] = (
        made[:, 2 * EDGE :] - fine(made[:, :EDGE], found[1]) - fine(made[:, EDGE : 2 * EDGE], found[2])
    )
    response = 0.0
    for i in range(size // EDGE):
        steer = steer_ref[pl.ds(i * EDGE, EDGE), :].astype(jnp.float32)
        response = response + jnp.sum(steer * found[i], axis=0, keepdims=True)
    for i in range(size // EDGE):
        out_ref[pl.ds(i * EDGE, EDGE), :] = (found[i] / response).astype(out_ref.dtype)


def make_weights(count, own, other, steering):
    size, beams = steering.shape
    smem = pl.BlockSpec(memory_space=pltpu.SMEM)
    vmem = pl.BlockSpec(memory_space=pltpu.VMEM)
    wide = 2 * EDGE + beams
    params = pltpu.CompilerParams(vmem_limit_bytes=VMEM_BYTES)
    minus = pl.pallas_call(
        corner_kernel,
        out_shape=jax.ShapeDtypeStruct((EDGE, EDGE), jnp.float32),
        in_specs=[smem, vmem, vmem],
        out_specs=vmem,
        compiler_params=params,
        cost_estimate=pl.CostEstimate(flops=10**9, bytes_accessed=10**6, transcendentals=0),
    )(count, own[0], other[0])
    made, less = pl.pallas_call(
        side_kernel,
        out_shape=[
            jax.ShapeDtypeStruct((EDGE, wide), jnp.float32),
            jax.ShapeDtypeStruct((2, EDGE, wide), jnp.float32),
        ],
        in_specs=[smem, vmem, vmem, vmem, vmem],
        out_specs=[vmem, vmem],
        compiler_params=params,
        cost_estimate=pl.CostEstimate(flops=10**9, bytes_accessed=10**6, transcendentals=0),
    )(count, own[1], other[1], steering, minus)
    return pl.pallas_call(
        late_kernel,
        out_shape=jax.ShapeDtypeStruct((size, beams), jnp.bfloat16),
        in_specs=[smem] + [vmem] * 7,
        out_specs=vmem,
        compiler_params=params,
        cost_estimate=pl.CostEstimate(flops=10**9, bytes_accessed=2 * 10**6, transcendentals=0),
    )(count, own[0], other[0], own[2], other[2], steering, made, less)


def split_kernel(which_ref, x_ref, out_ref):
    out_ref[:, 0] = x_ref[0]


def split(which, x):
    halves, group, rows, wide = x.shape
    chunks = 4
    return pl.pallas_call(
        split_kernel,
        out_shape=jax.ShapeDtypeStruct((group, halves, rows, wide), x.dtype),
        grid_spec=pltpu.PrefetchScalarGridSpec(
            num_scalar_prefetch=1,
            grid=(halves, chunks),
            in_specs=[
                pl.BlockSpec(
                    (1, group // chunks, rows, wide), lambda s, i, which: (which[s], i, 0, 0)
                )
            ],
            out_specs=pl.BlockSpec(
                (group // chunks, 1, rows, wide), lambda s, i, which: (i, s, 0, 0)
            ),
        ),
        compiler_params=pltpu.CompilerParams(vmem_limit_bytes=SPLIT_BYTES),
        cost_estimate=pl.CostEstimate(flops=0, bytes_accessed=2 * x.size, transcendentals=0),
    )(which, x)


def body(halves, snapshots, steering, train_list, train_count):
    bin_total, gate_rows, channels = snapshots.shape
    half = lax.axis_index("half").astype(jnp.int32)
    group = bin_total // halves
    order, base = jnp.stack([half, 1 - half]), half[None] * group
    peers = [(0, 1), (1, 0)]

    def exchange(x):
        return lax.all_to_all(x, INNER, split_axis=0, concat_axis=0, tiled=True)

    other_list = lax.ppermute(train_list, "half", peers)
    other_count = lax.ppermute(train_count, "half", peers)
    outgoing = split(order, snapshots.reshape(halves, group, gate_rows, channels))
    outgoing, other_list, other_count, base = lax.optimization_barrier(
        (outgoing, other_list, other_count, base)
    )
    blocks = exchange(outgoing)

    other_gram = partial_gram(1, base, other_list, other_count, blocks)
    arrived = [lax.ppermute(x, "half", peers) for x in other_gram]
    own_gram = partial_gram(0, base, train_list, train_count, blocks)
    weights = make_weights(train_count, own_gram, arrived, steering[0])
    other_weights = lax.ppermute(weights, "half", peers)

    def beams(x, w):
        made = jnp.einsum("ngd,de->nge", x, w, preferred_element_type=jnp.float32)
        return made.astype(jnp.bfloat16)

    made = jnp.stack([beams(blocks[:, 0], weights), beams(blocks[:, 1], other_weights)], axis=1)
    made, here, there = lax.optimization_barrier((made, half, 1 - half))
    out = jnp.moveaxis(exchange(made), 1, 0)
    sets = [
        lax.dynamic_index_in_dim(out, at, 0, keepdims=False, allow_negative_indices=False)
        for at in (here, there)
    ]
    return jnp.concatenate(sets, axis=0)


def solution(mesh):
    ranges, dopplers = mesh.devices.shape
    halves = 2
    cut = Mesh(mesh.devices.reshape(halves, ranges // halves, dopplers), EVERY)

    def run(*args):
        return body(halves, *args)

    return jax.shard_map(
        run,
        mesh=cut,
        in_specs=(P(None, EVERY, None), P(EVERY, None, None), P(EVERY, None), P(EVERY)),
        out_specs=P(None, EVERY, None),
        check_vma=False,
    )
```

```python
import functools

import jax
import jax.numpy as jnp
from jax import lax
from jax.experimental import pallas as pl
from jax.experimental.pallas import tpu as pltpu
from jax.sharding import Mesh
from jax.sharding import PartitionSpec as P

BLOCK = 128
LOADING = 0.1
EDGE = 128
STEP = 16
PACKED = (EDGE, 2 * EDGE + 8, EDGE + EDGE // 2)
INNER = ("inner", "doppler")
EVERY = ("half",) + INNER
VMEM_BYTES = 16 * 1024 * 1024
SPLIT_BYTES = 16 * 1024 * 1024


def edge_iota(dim, rows=EDGE):
    return lax.broadcasted_iota(jnp.int32, (rows, EDGE), dim)


def gram_kernel(which, base_ref, list_ref, count_ref, blocks_ref, corner_ref, side_ref, late_ref, chosen):
    group, _, rows, size = blocks_ref.shape
    for p in range(list_ref.shape[1]):
        chosen[list_ref[0, p]] = (p < count_ref[0]).astype(jnp.int32)
    every = [blocks_ref[n, which] for n in range(group)]
    kept = [
        jnp.where(chosen[base_ref[0] + n] > 0, x, jnp.zeros_like(x)) for n, x in enumerate(every)
    ]
    every = jnp.concatenate(every, axis=0)
    kept = jnp.concatenate(kept, axis=0)

    def strip(i):
        return lax.dot_general(
            kept[:, i * EDGE : (i + 1) * EDGE], every[:, i * EDGE :], (((0,), (0,)), ((), ())),
            preferred_element_type=jnp.float32,
        )

    half = EDGE // 2
    r, c = edge_iota(0), edge_iota(1)
    zero, one, two = strip(0), strip(1), strip(2)
    corner_ref[...] = jnp.where(r <= c, zero[:, :EDGE], one[:, :EDGE])
    side_ref[pl.ds(0, EDGE), :] = zero[:, EDGE : 2 * EDGE]
    side_ref[pl.ds(EDGE, EDGE), :] = zero[:, 2 * EDGE :]
    late_ref[pl.ds(0, EDGE), :] = one[:, EDGE:]
    low = pltpu.roll(two[half:], half, axis=1)
    rh, ch = r[:half], c[:half]
    late_ref[pl.ds(EDGE, half), :] = jnp.where((ch < half) & (rh > ch), low, two[:half])
    first = jnp.sum(jnp.where(r == c, one[:, :EDGE], 0.0), axis=0, keepdims=True)
    second = jnp.sum(jnp.where(rh == ch, low, 0.0), axis=0, keepdims=True)
    s = edge_iota(0, 8)
    side_ref[pl.ds(2 * EDGE, 8), :] = jnp.where(s == 0, first, jnp.where(s == 1, second, 0.0))


def partial_gram(which, base, lists, counts, blocks):
    group, _, rows, size = blocks.shape
    smem = pl.BlockSpec(memory_space=pltpu.SMEM)
    vmem = pl.BlockSpec(memory_space=pltpu.VMEM)
    return pl.pallas_call(
        functools.partial(gram_kernel, which),
        out_shape=[jax.ShapeDtypeStruct((n, EDGE), jnp.float32) for n in PACKED],
        in_specs=[smem, smem, smem, vmem],
        out_specs=[vmem] * len(PACKED),
        scratch_shapes=[pltpu.SMEM((lists.shape[1],), jnp.int32)],
        compiler_params=pltpu.CompilerParams(vmem_limit_bytes=3 * VMEM_BYTES),
        cost_estimate=pl.CostEstimate(
            flops=2 * group * rows * size * size,
            bytes_accessed=2 * group * rows * size,
            transcendentals=0,
        ),
    )(base, lists, counts, blocks)


def unpack_late(late, diag):
    half = EDGE // 2
    r, c = edge_iota(0, half), edge_iota(1, half)
    top = late[EDGE:]
    side = jnp.concatenate([top, jnp.zeros_like(top)], axis=0).T
    upper = jnp.where((c < half) & (r > c), side[:half], top)
    low = jnp.where(r > c, top, jnp.where(r < c, side[:half], diag))
    lower = jnp.where(c < half, side[half:], pltpu.roll(low, half, axis=1))
    return late[:EDGE], jnp.concatenate([upper, lower], axis=0)


def fine(a, b, dims=(((1,), (0,)), ((), ()))):
    return lax.dot_general(
        a, b, dims, precision=lax.Precision.HIGHEST, preferred_element_type=jnp.float32
    )


def thirds(x):
    hi = x.astype(jnp.bfloat16)
    rest = x - hi.astype(jnp.float32)
    mid = rest.astype(jnp.bfloat16)
    low = (rest - mid.astype(jnp.float32)).astype(jnp.bfloat16)
    return hi, mid, low


def outer(a, b):
    ah, am, al = thirds(a)
    bh, bm, bl = thirds(b)
    left = jnp.concatenate([ah, ah, ah, am, am, al], axis=0)
    right = jnp.concatenate([bh, bm, bl, bh, bm, bh], axis=0)
    return lax.dot_general(
        left, right, (((0,), (0,)), ((), ())), preferred_element_type=jnp.float32
    )


def eliminate(rows, cols):
    full = (STEP, EDGE)
    sub = lax.broadcasted_iota(jnp.int32, full, 0)

    def row(x, k):
        return jnp.broadcast_to(x[k : k + 1], full)

    cols = list(cols)
    for k in range(0, STEP, 2):
        one, two = sub == k, sub == k + 1
        here = one | two
        a, b, c = row(cols[k], k), row(cols[k + 1], k), row(cols[k + 1], k + 1)
        inv = 1.0 / (a * c - b * b)
        first = jnp.where(one, 1.0, jnp.where(two, 0.0, -cols[k]))
        second = jnp.where(two, 1.0, jnp.where(one, 0.0, -cols[k + 1]))

        left = (first * c - second * b) * inv
        after = (second * a - first * b) * inv

        def step(x):
            r, s = row(x, k), row(x, k + 1)
            return jnp.where(here, 0.0, x) + (left * r + after * s)

        for i in range(k + 2, STEP):
            cols[i] = step(cols[i])
        rows = step(rows)
    return rows


def negative_inverse(strips):
    full = (STEP, EDGE)
    panels = EDGE // STEP
    sub = lax.broadcasted_iota(jnp.int32, full, 0)
    lane = lax.broadcasted_iota(jnp.int32, full, 1)

    def spread(x, at):
        return [
            jnp.take_along_axis(
                x, jnp.full(full, at + i, jnp.int32), axis=1, mode="promise_in_bounds"
            )
            for i in range(STEP)
        ]

    rows = strips[0]
    for p in range(panels):
        at = p * STEP
        inside = (lane >= at) & (lane < at + STEP)
        swept = jnp.where(inside, jnp.where(lane == sub + at, -1.0, 0.0), rows)
        weights = spread(strips[p + 1], at) if p + 1 < panels else None
        solved = eliminate(swept, spread(rows, at))
        if weights is not None:
            terms = [w * jnp.broadcast_to(solved[k : k + 1], full) for k, w in enumerate(weights)]
            while len(terms) > 1:
                terms = [x + y for x, y in zip(terms[::2], terms[1::2])]
            rows = jnp.where(inside, 0.0, strips[p + 1]) - terms[0]
        change = outer(swept, solved)
        strips = [
            rows
            if q == p + 1
            else (jnp.zeros(full, jnp.float32) if q == p else jnp.where(inside, 0.0, strips[q]))
            - change[q * STEP : (q + 1) * STEP]
            for q in range(panels)
        ]
    return jnp.concatenate(strips, axis=0)


TURNED = (((0,), (0,)), ((), ()))


def inverse_scale(count_ref):
    return 1.0 / (BLOCK * count_ref[0]).astype(jnp.float32)


def loading():
    return jnp.where(edge_iota(0) == edge_iota(1), LOADING, 0.0)


def minus_inverse(block):
    return negative_inverse([block[q : q + STEP] for q in range(0, EDGE, STEP)])


def corner_kernel(count_ref, own_ref, other_ref, minus_ref):
    both = own_ref[...] + other_ref[...]
    block = jnp.where(edge_iota(0) <= edge_iota(1), both, both.T)
    minus_ref[...] = minus_inverse(block * inverse_scale(count_ref) + loading())


def side_kernel(
    count_ref, own_corner, other_corner, own_ref, other_ref, steer_ref, minus_ref,
    made_ref, less_ref, next_ref,
):
    inv_scale = inverse_scale(count_ref)
    side = own_ref[...] + other_ref[...]
    near, far = side[:EDGE] * inv_scale, side[EDGE : 2 * EDGE] * inv_scale
    minus = minus_ref[...]
    r, c = edge_iota(0), edge_iota(1)
    both = own_corner[...] + other_corner[...]
    diag = side[2 * EDGE : 2 * EDGE + 1]
    block = jnp.where(r > c, both, jnp.where(r < c, both.T, diag)) * inv_scale + loading()
    close = -fine(minus, near)
    taken = fine(near, close, TURNED)
    next_ref[...] = minus_inverse(block - taken)
    right = steer_ref[pl.ds(0, EDGE), :].astype(jnp.float32)
    made = -fine(minus, jnp.concatenate([far, right], axis=1))
    made_ref[:, :EDGE] = close
    made_ref[:, EDGE:] = made
    less_ref[0] = fine(near, made, TURNED)
    less_ref[1] = fine(far, made, TURNED)


def late_kernel(
    count_ref, own_late, other_late, own_side, other_side, steer_ref, made_ref, less_ref,
    minus_ref, out_ref,
):
    size, beams = steer_ref.shape
    parts = size // EDGE
    inv_scale = inverse_scale(count_ref)
    diag = own_side[pl.ds(2 * EDGE, 8), :] + other_side[pl.ds(2 * EDGE, 8), :]
    near, block = unpack_late(own_late[...] + other_late[...], diag[1:2])
    near = near * inv_scale - less_ref[0, :, :EDGE]
    block = block * inv_scale + loading() - less_ref[1, :, :EDGE]
    minus = minus_ref[...]
    step = -fine(minus, near)
    block = block - fine(near, step, TURNED)
    right = [
        steer_ref[pl.ds(i * EDGE, EDGE), :].astype(jnp.float32) - less_ref[i - 1, :, EDGE:]
        for i in (1, 2)
    ]
    middle = -fine(minus, right[0])
    last = right[1] - fine(near, middle, TURNED)
    made = made_ref[...]
    close, far, right = made[:, :EDGE], made[:, EDGE : 2 * EDGE], made[:, 2 * EDGE :]
    base = jnp.concatenate([right - fine(close, middle), middle], axis=0)
    turn = jnp.concatenate([far - fine(close, step), step], axis=0)
    x = -fine(minus_inverse(block), last)
    found = jnp.concatenate([base - fine(turn, x), x], axis=0)
    response = jnp.sum(steer_ref[...].astype(jnp.float32) * found, axis=0, keepdims=True)
    out_ref[...] = (found / response).astype(out_ref.dtype)


def make_weights(count, own, other, steering):
    size, beams = steering.shape
    smem = pl.BlockSpec(memory_space=pltpu.SMEM)
    vmem = pl.BlockSpec(memory_space=pltpu.VMEM)
    wide = EDGE + beams
    square = jax.ShapeDtypeStruct((EDGE, EDGE), jnp.float32)

    def call(kernel, out_shape, *args):
        return pl.pallas_call(
            kernel,
            out_shape=out_shape,
            in_specs=[smem] + [vmem] * len(args),
            out_specs=jax.tree.map(lambda _: vmem, out_shape),
            compiler_params=pltpu.CompilerParams(vmem_limit_bytes=VMEM_BYTES),
            cost_estimate=pl.CostEstimate(flops=10**9, bytes_accessed=10**6, transcendentals=0),
        )(count, *args)

    corner = call(corner_kernel, square, own[0], other[0])
    made, less, second = call(
        side_kernel,
        [
            jax.ShapeDtypeStruct((EDGE, EDGE + wide), jnp.float32),
            jax.ShapeDtypeStruct((2, EDGE, wide), jnp.float32),
            square,
        ],
        own[0], other[0], own[1], other[1], steering, corner,
    )
    return call(
        late_kernel,
        jax.ShapeDtypeStruct((size, beams), jnp.bfloat16),
        own[2], other[2], own[1], other[1], steering, made, less, second,
    )


def split_kernel(which_ref, x_ref, out_ref):
    out_ref[:, 0] = x_ref[0]


def split(which, x):
    halves, group, rows, wide = x.shape
    chunks = 4
    return pl.pallas_call(
        split_kernel,
        out_shape=jax.ShapeDtypeStruct((group, halves, rows, wide), x.dtype),
        grid_spec=pltpu.PrefetchScalarGridSpec(
            num_scalar_prefetch=1,
            grid=(halves, chunks),
            in_specs=[
                pl.BlockSpec(
                    (1, group // chunks, rows, wide), lambda s, i, which: (which[s], i, 0, 0)
                )
            ],
            out_specs=pl.BlockSpec(
                (group // chunks, 1, rows, wide), lambda s, i, which: (i, s, 0, 0)
            ),
        ),
        compiler_params=pltpu.CompilerParams(vmem_limit_bytes=SPLIT_BYTES),
        cost_estimate=pl.CostEstimate(flops=0, bytes_accessed=2 * x.size, transcendentals=0),
    )(which, x)


def body(halves, snapshots, steering, train_list, train_count):
    bin_total, gate_rows, channels = snapshots.shape
    half = lax.axis_index("half").astype(jnp.int32)
    group = bin_total // halves
    order, base = jnp.stack([half, 1 - half]), half[None] * group
    peers = [(0, 1), (1, 0)]

    def exchange(x):
        return lax.all_to_all(x, INNER, split_axis=0, concat_axis=0, tiled=True)

    other_list = lax.ppermute(train_list, "half", peers)
    other_count = lax.ppermute(train_count, "half", peers)
    outgoing = split(order, snapshots.reshape(halves, group, gate_rows, channels))
    outgoing, other_list, other_count, base = lax.optimization_barrier(
        (outgoing, other_list, other_count, base)
    )
    blocks = exchange(outgoing)

    other_gram = partial_gram(1, base, other_list, other_count, blocks)
    arrived = [lax.ppermute(x, "half", peers) for x in other_gram]
    own_gram = partial_gram(0, base, train_list, train_count, blocks)
    weights = make_weights(train_count, own_gram, arrived, steering[0])
    other_weights = lax.ppermute(weights, "half", peers)

    def beams(x, w):
        made = jnp.einsum("ngd,de->nge", x, w, preferred_element_type=jnp.float32)
        return made.astype(jnp.bfloat16)

    made = jnp.stack([beams(blocks[:, 0], weights), beams(blocks[:, 1], other_weights)], axis=1)
    made, here, there = lax.optimization_barrier((made, half, 1 - half))
    out = jnp.moveaxis(exchange(made), 1, 0)
    sets = [
        lax.dynamic_index_in_dim(out, at, 0, keepdims=False, allow_negative_indices=False)
        for at in (here, there)
    ]
    return jnp.concatenate(sets, axis=0)


def solution(mesh):
    ranges, dopplers = mesh.devices.shape
    halves = 2
    cut = Mesh(mesh.devices.reshape(halves, ranges // halves, dopplers), EVERY)

    def run(*args):
        return body(halves, *args)

    return jax.shard_map(
        run,
        mesh=cut,
        in_specs=(P(None, EVERY, None), P(EVERY, None, None), P(EVERY, None), P(EVERY)),
        out_specs=P(None, EVERY, None),
        check_vma=False,
    )
```

```python
import functools

import jax
import jax.numpy as jnp
from jax import lax
from jax.experimental import pallas as pl
from jax.experimental.pallas import tpu as pltpu
from jax.sharding import Mesh
from jax.sharding import PartitionSpec as P

BLOCK = 128
LOADING = 0.1
EDGE = 128
STEP = 16
PACKED = (EDGE, 2 * EDGE + 8, EDGE + EDGE // 2)
INNER = ("inner", "doppler")
EVERY = ("half",) + INNER
VMEM_BYTES = 16 * 1024 * 1024
SPLIT_BYTES = 16 * 1024 * 1024


def edge_iota(dim, rows=EDGE):
    return lax.broadcasted_iota(jnp.int32, (rows, EDGE), dim)


def gram_kernel(which, base_ref, list_ref, count_ref, blocks_ref, corner_ref, side_ref, late_ref, chosen):
    group, _, rows, size = blocks_ref.shape
    for p in range(list_ref.shape[1]):
        chosen[list_ref[0, p]] = (p < count_ref[0]).astype(jnp.int32)
    every = [blocks_ref[n, which] for n in range(group)]
    kept = [
        jnp.where(chosen[base_ref[0] + n] > 0, x, jnp.zeros_like(x)) for n, x in enumerate(every)
    ]
    every = jnp.concatenate(every, axis=0)
    kept = jnp.concatenate(kept, axis=0)

    def strip(i):
        return lax.dot_general(
            kept[:, i * EDGE : (i + 1) * EDGE], every[:, i * EDGE :], (((0,), (0,)), ((), ())),
            preferred_element_type=jnp.float32,
        )

    half = EDGE // 2
    r, c = edge_iota(0), edge_iota(1)
    zero, one, two = strip(0), strip(1), strip(2)
    corner_ref[...] = jnp.where(r <= c, zero[:, :EDGE], one[:, :EDGE])
    side_ref[pl.ds(0, EDGE), :] = zero[:, EDGE : 2 * EDGE]
    side_ref[pl.ds(EDGE, EDGE), :] = zero[:, 2 * EDGE :]
    late_ref[pl.ds(0, EDGE), :] = one[:, EDGE:]
    low = pltpu.roll(two[half:], half, axis=1)
    rh, ch = r[:half], c[:half]
    late_ref[pl.ds(EDGE, half), :] = jnp.where((ch < half) & (rh > ch), low, two[:half])
    first = jnp.sum(jnp.where(r == c, one[:, :EDGE], 0.0), axis=0, keepdims=True)
    second = jnp.sum(jnp.where(rh == ch, low, 0.0), axis=0, keepdims=True)
    s = edge_iota(0, 8)
    side_ref[pl.ds(2 * EDGE, 8), :] = jnp.where(s == 0, first, jnp.where(s == 1, second, 0.0))


def partial_gram(which, base, lists, counts, blocks):
    group, _, rows, size = blocks.shape
    smem = pl.BlockSpec(memory_space=pltpu.SMEM)
    vmem = pl.BlockSpec(memory_space=pltpu.VMEM)
    return pl.pallas_call(
        functools.partial(gram_kernel, which),
        out_shape=[jax.ShapeDtypeStruct((n, EDGE), jnp.float32) for n in PACKED],
        in_specs=[smem, smem, smem, vmem],
        out_specs=[vmem] * len(PACKED),
        scratch_shapes=[pltpu.SMEM((lists.shape[1],), jnp.int32)],
        compiler_params=pltpu.CompilerParams(vmem_limit_bytes=3 * VMEM_BYTES),
        cost_estimate=pl.CostEstimate(
            flops=2 * group * rows * size * size,
            bytes_accessed=2 * group * rows * size,
            transcendentals=0,
        ),
    )(base, lists, counts, blocks)


def unpack_late(late, diag):
    half = EDGE // 2
    r, c = edge_iota(0, half), edge_iota(1, half)
    top = late[EDGE:]
    side = jnp.concatenate([top, jnp.zeros_like(top)], axis=0).T
    upper = jnp.where((c < half) & (r > c), side[:half], top)
    low = jnp.where(r > c, top, jnp.where(r < c, side[:half], diag))
    lower = jnp.where(c < half, side[half:], pltpu.roll(low, half, axis=1))
    return late[:EDGE], jnp.concatenate([upper, lower], axis=0)


def fine(a, b, dims=(((1,), (0,)), ((), ()))):
    return lax.dot_general(
        a, b, dims, precision=lax.Precision.HIGHEST, preferred_element_type=jnp.float32
    )


def thirds(x):
    hi = x.astype(jnp.bfloat16)
    rest = x - hi.astype(jnp.float32)
    mid = rest.astype(jnp.bfloat16)
    low = (rest - mid.astype(jnp.float32)).astype(jnp.bfloat16)
    return hi, mid, low


def outer(a, b):
    ah, am, al = thirds(a)
    bh, bm, bl = thirds(b)
    left = jnp.concatenate([ah, ah, ah, am, am, al], axis=0)
    right = jnp.concatenate([bh, bm, bl, bh, bm, bh], axis=0)
    return lax.dot_general(
        left, right, (((0,), (0,)), ((), ())), preferred_element_type=jnp.float32
    )


def eliminate(rows, cols):
    full = (STEP, EDGE)
    sub = lax.broadcasted_iota(jnp.int32, full, 0)

    def row(x, k):
        return jnp.broadcast_to(x[k : k + 1], full)

    cols = list(cols)
    for k in range(0, STEP, 2):
        one, two = sub == k, sub == k + 1
        here = one | two
        a, b, c = row(cols[k], k), row(cols[k + 1], k), row(cols[k + 1], k + 1)
        inv = 1.0 / (a * c - b * b)
        first = jnp.where(one, 1.0, jnp.where(two, 0.0, -cols[k]))
        second = jnp.where(two, 1.0, jnp.where(one, 0.0, -cols[k + 1]))

        left = (first * c - second * b) * inv
        after = (second * a - first * b) * inv

        def step(x):
            r, s = row(x, k), row(x, k + 1)
            return jnp.where(here, 0.0, x) + (left * r + after * s)

        for i in range(k + 2, STEP):
            cols[i] = step(cols[i])
        rows = step(rows)
    return rows


def negative_inverse(strips, beside=()):
    full = (STEP, EDGE)
    panels = EDGE // STEP
    sub = lax.broadcasted_iota(jnp.int32, full, 0)
    lane = lax.broadcasted_iota(jnp.int32, full, 1)

    def spread(x, at):
        return [
            jnp.take_along_axis(
                x, jnp.full(full, at + i, jnp.int32), axis=1, mode="promise_in_bounds"
            )
            for i in range(STEP)
        ]

    rows = strips[0]
    for p in range(panels):
        at = p * STEP
        inside = (lane >= at) & (lane < at + STEP)
        swept = jnp.where(inside, jnp.where(lane == sub + at, -1.0, 0.0), rows)
        weights = spread(strips[p + 1], at) if p + 1 < panels else None
        solved = eliminate(swept, spread(rows, at))
        if weights is not None:
            terms = [w * jnp.broadcast_to(solved[k : k + 1], full) for k, w in enumerate(weights)]
            while len(terms) > 1:
                terms = [x + y for x, y in zip(terms[::2], terms[1::2])]
            rows = jnp.where(inside, 0.0, strips[p + 1]) - terms[0]
        change = outer(swept, solved)
        if p < len(beside):
            beside[p]()
        strips = [
            rows
            if q == p + 1
            else (jnp.zeros(full, jnp.float32) if q == p else jnp.where(inside, 0.0, strips[q]))
            - change[q * STEP : (q + 1) * STEP]
            for q in range(panels)
        ]
    return jnp.concatenate(strips, axis=0)


TURNED = (((0,), (0,)), ((), ()))


def inverse_scale(count_ref):
    return 1.0 / (BLOCK * count_ref[0]).astype(jnp.float32)


def loading():
    return jnp.where(edge_iota(0) == edge_iota(1), LOADING, 0.0)


def minus_inverse(block, beside=()):
    return negative_inverse([block[q : q + STEP] for q in range(0, EDGE, STEP)], beside)


def corner_kernel(count_ref, own_ref, other_ref, minus_ref):
    both = own_ref[...] + other_ref[...]
    block = jnp.where(edge_iota(0) <= edge_iota(1), both, both.T)
    minus_ref[...] = minus_inverse(block * inverse_scale(count_ref) + loading())


def side_kernel(
    count_ref, own_corner, other_corner, own_ref, other_ref, steer_ref, minus_ref,
    made_ref, less_ref, next_ref,
):
    inv_scale = inverse_scale(count_ref)
    side = own_ref[...] + other_ref[...]
    near, far = side[:EDGE] * inv_scale, side[EDGE : 2 * EDGE] * inv_scale
    minus = minus_ref[...]
    r, c = edge_iota(0), edge_iota(1)
    both = own_corner[...] + other_corner[...]
    diag = side[2 * EDGE : 2 * EDGE + 1]
    block = jnp.where(r > c, both, jnp.where(r < c, both.T, diag)) * inv_scale + loading()
    close = -fine(minus, near)
    block = block - fine(near, close, TURNED)
    made_ref[:, :EDGE] = close
    right = steer_ref[pl.ds(0, EDGE), :].astype(jnp.float32)
    made = {}

    def solve(name, x, at):
        made[name] = -fine(minus, x)
        made_ref[:, at : at + x.shape[1]] = made[name]

    def take(i, lhs, name, at):
        less_ref[i, :, at : at + made[name].shape[1]] = fine(lhs, made[name], TURNED)

    next_ref[...] = minus_inverse(
        block,
        [
            lambda: solve("far", far, EDGE),
            lambda: solve("right", right, 2 * EDGE),
            lambda: take(0, near, "far", 0),
            lambda: take(1, far, "far", 0),
            lambda: take(0, near, "right", EDGE),
            lambda: take(1, far, "right", EDGE),
        ],
    )


def late_kernel(
    count_ref, own_late, other_late, own_side, other_side, steer_ref, made_ref, less_ref,
    minus_ref, out_ref,
):
    size, beams = steer_ref.shape
    parts = size // EDGE
    inv_scale = inverse_scale(count_ref)
    diag = own_side[pl.ds(2 * EDGE, 8), :] + other_side[pl.ds(2 * EDGE, 8), :]
    near, block = unpack_late(own_late[...] + other_late[...], diag[1:2])
    near = near * inv_scale - less_ref[0, :, :EDGE]
    block = block * inv_scale + loading() - less_ref[1, :, :EDGE]
    minus = minus_ref[...]
    step = -fine(minus, near)
    block = block - fine(near, step, TURNED)
    right = [
        steer_ref[pl.ds(i * EDGE, EDGE), :].astype(jnp.float32) - less_ref[i - 1, :, EDGE:]
        for i in (1, 2)
    ]
    made = made_ref[...]
    close, far, top = made[:, :EDGE], made[:, EDGE : 2 * EDGE], made[:, 2 * EDGE :]
    got = {}

    def middle():
        got["middle"] = -fine(minus, right[0])

    def last():
        got["last"] = right[1] - fine(near, got["middle"], TURNED)

    def base():
        got["base"] = jnp.concatenate([top - fine(close, got["middle"]), got["middle"]], axis=0)

    def turn():
        got["turn"] = jnp.concatenate([far - fine(close, step), step], axis=0)

    x = -fine(minus_inverse(block, [middle, last, base, turn]), got["last"])
    base, turn = got["base"], got["turn"]
    found = jnp.concatenate([base - fine(turn, x), x], axis=0)
    response = jnp.sum(steer_ref[...].astype(jnp.float32) * found, axis=0, keepdims=True)
    out_ref[...] = (found * (1.0 / response)).astype(out_ref.dtype)


def make_weights(count, own, other, steering):
    size, beams = steering.shape
    smem = pl.BlockSpec(memory_space=pltpu.SMEM)
    vmem = pl.BlockSpec(memory_space=pltpu.VMEM)
    wide = EDGE + beams
    square = jax.ShapeDtypeStruct((EDGE, EDGE), jnp.float32)

    def call(kernel, out_shape, *args):
        return pl.pallas_call(
            kernel,
            out_shape=out_shape,
            in_specs=[smem] + [vmem] * len(args),
            out_specs=jax.tree.map(lambda _: vmem, out_shape),
            compiler_params=pltpu.CompilerParams(vmem_limit_bytes=VMEM_BYTES),
            cost_estimate=pl.CostEstimate(flops=10**9, bytes_accessed=10**6, transcendentals=0),
        )(count, *args)

    corner = call(corner_kernel, square, own[0], other[0])
    made, less, second = call(
        side_kernel,
        [
            jax.ShapeDtypeStruct((EDGE, EDGE + wide), jnp.float32),
            jax.ShapeDtypeStruct((2, EDGE, wide), jnp.float32),
            square,
        ],
        own[0], other[0], own[1], other[1], steering, corner,
    )
    return call(
        late_kernel,
        jax.ShapeDtypeStruct((size, beams), jnp.bfloat16),
        own[2], other[2], own[1], other[1], steering, made, less, second,
    )


def split_kernel(which_ref, x_ref, out_ref):
    out_ref[:, 0] = x_ref[0]


def split(which, x):
    halves, group, rows, wide = x.shape
    chunks = 4
    return pl.pallas_call(
        split_kernel,
        out_shape=jax.ShapeDtypeStruct((group, halves, rows, wide), x.dtype),
        grid_spec=pltpu.PrefetchScalarGridSpec(
            num_scalar_prefetch=1,
            grid=(halves, chunks),
            in_specs=[
                pl.BlockSpec(
                    (1, group // chunks, rows, wide), lambda s, i, which: (which[s], i, 0, 0)
                )
            ],
            out_specs=pl.BlockSpec(
                (group // chunks, 1, rows, wide), lambda s, i, which: (i, s, 0, 0)
            ),
        ),
        compiler_params=pltpu.CompilerParams(vmem_limit_bytes=SPLIT_BYTES),
        cost_estimate=pl.CostEstimate(flops=0, bytes_accessed=2 * x.size, transcendentals=0),
    )(which, x)


def body(halves, snapshots, steering, train_list, train_count):
    bin_total, gate_rows, channels = snapshots.shape
    half = lax.axis_index("half").astype(jnp.int32)
    group = bin_total // halves
    order, base = jnp.stack([half, 1 - half]), half[None] * group
    peers = [(0, 1), (1, 0)]

    def exchange(x):
        return lax.all_to_all(x, INNER, split_axis=0, concat_axis=0, tiled=True)

    other_list = lax.ppermute(train_list, "half", peers)
    other_count = lax.ppermute(train_count, "half", peers)
    outgoing = split(order, snapshots.reshape(halves, group, gate_rows, channels))
    outgoing, other_list, other_count, base = lax.optimization_barrier(
        (outgoing, other_list, other_count, base)
    )
    blocks = exchange(outgoing)

    other_gram = partial_gram(1, base, other_list, other_count, blocks)
    arrived = [lax.ppermute(x, "half", peers) for x in other_gram]
    own_gram = partial_gram(0, base, train_list, train_count, blocks)
    weights = make_weights(train_count, own_gram, arrived, steering[0])
    other_weights = lax.ppermute(weights, "half", peers)

    def beams(x, w):
        made = jnp.einsum("ngd,de->nge", x, w, preferred_element_type=jnp.float32)
        return made.astype(jnp.bfloat16)

    made = jnp.stack([beams(blocks[:, 0], weights), beams(blocks[:, 1], other_weights)], axis=1)
    made, here, there = lax.optimization_barrier((made, half, 1 - half))
    out = jnp.moveaxis(exchange(made), 1, 0)
    sets = [
        lax.dynamic_index_in_dim(out, at, 0, keepdims=False, allow_negative_indices=False)
        for at in (here, there)
    ]
    return jnp.concatenate(sets, axis=0)


def solution(mesh):
    ranges, dopplers = mesh.devices.shape
    halves = 2
    cut = Mesh(mesh.devices.reshape(halves, ranges // halves, dopplers), EVERY)

    def run(*args):
        return body(halves, *args)

    return jax.shard_map(
        run,
        mesh=cut,
        in_specs=(P(None, EVERY, None), P(EVERY, None, None), P(EVERY, None), P(EVERY)),
        out_specs=P(None, EVERY, None),
        check_vma=False,
    )
```

```python
import functools

import jax
import jax.numpy as jnp
from jax import lax
from jax.experimental import pallas as pl
from jax.experimental.pallas import tpu as pltpu
from jax.sharding import Mesh
from jax.sharding import PartitionSpec as P

BLOCK = 128
LOADING = 0.1
EDGE = 128
STEP = 16
PACKED = (EDGE, 2 * EDGE + 8, EDGE + EDGE // 2)
INNER = ("inner", "doppler")
EVERY = ("half",) + INNER
VMEM_BYTES = 16 * 1024 * 1024
TURNED = (((0,), (0,)), ((), ()))
SPLIT_BYTES = 16 * 1024 * 1024


def edge_iota(dim, rows=EDGE):
    return lax.broadcasted_iota(jnp.int32, (rows, EDGE), dim)


def gram_kernel(which, base_ref, list_ref, count_ref, blocks_ref, corner_ref, side_ref, late_ref, chosen):
    group, _, rows, size = blocks_ref.shape
    for p in range(list_ref.shape[1]):
        chosen[list_ref[0, p]] = (p < count_ref[0]).astype(jnp.int32)
    every = [blocks_ref[n, which] for n in range(group)]
    kept = [
        jnp.where(chosen[base_ref[0] + n] > 0, x, jnp.zeros_like(x)) for n, x in enumerate(every)
    ]
    every = jnp.concatenate(every, axis=0)
    kept = jnp.concatenate(kept, axis=0)

    def strip(i):
        return lax.dot_general(
            kept[:, i * EDGE : (i + 1) * EDGE], every[:, i * EDGE :], (((0,), (0,)), ((), ())),
            preferred_element_type=jnp.float32,
        )

    half = EDGE // 2
    r, c = edge_iota(0), edge_iota(1)
    zero, one, two = strip(0), strip(1), strip(2)
    corner_ref[...] = jnp.where(r <= c, zero[:, :EDGE], one[:, :EDGE])
    side_ref[pl.ds(0, EDGE), :] = zero[:, EDGE : 2 * EDGE]
    side_ref[pl.ds(EDGE, EDGE), :] = zero[:, 2 * EDGE :]
    late_ref[pl.ds(0, EDGE), :] = one[:, EDGE:]
    low = pltpu.roll(two[half:], half, axis=1)
    rh, ch = r[:half], c[:half]
    late_ref[pl.ds(EDGE, half), :] = jnp.where((ch < half) & (rh > ch), low, two[:half])
    first = jnp.sum(jnp.where(r == c, one[:, :EDGE], 0.0), axis=0, keepdims=True)
    second = jnp.sum(jnp.where(rh == ch, low, 0.0), axis=0, keepdims=True)
    s = edge_iota(0, 8)
    side_ref[pl.ds(2 * EDGE, 8), :] = jnp.where(s == 0, first, jnp.where(s == 1, second, 0.0))


def partial_gram(which, base, lists, counts, blocks):
    group, _, rows, size = blocks.shape
    smem = pl.BlockSpec(memory_space=pltpu.SMEM)
    vmem = pl.BlockSpec(memory_space=pltpu.VMEM)
    return pl.pallas_call(
        functools.partial(gram_kernel, which),
        out_shape=[jax.ShapeDtypeStruct((n, EDGE), jnp.float32) for n in PACKED],
        in_specs=[smem, smem, smem, vmem],
        out_specs=[vmem] * len(PACKED),
        scratch_shapes=[pltpu.SMEM((lists.shape[1],), jnp.int32)],
        compiler_params=pltpu.CompilerParams(vmem_limit_bytes=3 * VMEM_BYTES),
        cost_estimate=pl.CostEstimate(
            flops=2 * group * rows * size * size,
            bytes_accessed=2 * group * rows * size,
            transcendentals=0,
        ),
    )(base, lists, counts, blocks)


def unpack_late(late, diag):
    half = EDGE // 2
    r, c = edge_iota(0, half), edge_iota(1, half)
    top = late[EDGE:]
    side = jnp.concatenate([top, jnp.zeros_like(top)], axis=0).T
    upper = jnp.where((c < half) & (r > c), side[:half], top)
    low = jnp.where(r > c, top, jnp.where(r < c, side[:half], diag))
    lower = jnp.where(c < half, side[half:], pltpu.roll(low, half, axis=1))
    return late[:EDGE], jnp.concatenate([upper, lower], axis=0)


def thirds(x):
    hi = x.astype(jnp.bfloat16)
    rest = x - hi.astype(jnp.float32)
    mid = rest.astype(jnp.bfloat16)
    low = (rest - mid.astype(jnp.float32)).astype(jnp.bfloat16)
    return hi, mid, low


def fine(a, b, dims=(((1,), (0,)), ((), ()))):
    ah, am, al = thirds(a)
    bh, bm, bl = thirds(b)
    left = jnp.concatenate([ah, ah, ah, am, am, al], axis=dims[0][0][0])
    right = jnp.concatenate([bh, bm, bl, bh, bm, bh], axis=dims[0][1][0])
    return lax.dot_general(left, right, dims, preferred_element_type=jnp.float32)


def eliminate(rows, cols):
    full = (STEP, EDGE)
    sub = lax.broadcasted_iota(jnp.int32, full, 0)

    def row(x, k):
        return jnp.broadcast_to(x[k : k + 1], full)

    cols = list(cols)
    for k in range(0, STEP, 2):
        one, two = sub == k, sub == k + 1
        here = one | two
        a, b, c = row(cols[k], k), row(cols[k + 1], k), row(cols[k + 1], k + 1)
        inv = 1.0 / (a * c - b * b)
        first = jnp.where(one, 1.0, jnp.where(two, 0.0, -cols[k]))
        second = jnp.where(two, 1.0, jnp.where(one, 0.0, -cols[k + 1]))

        left = (first * c - second * b) * inv
        after = (second * a - first * b) * inv

        def step(x):
            r, s = row(x, k), row(x, k + 1)
            return jnp.where(here, 0.0, x) + (left * r + after * s)

        for i in range(k + 2, STEP):
            cols[i] = step(cols[i])
        rows = step(rows)
    return rows


def negative_inverse(strips, beside=()):
    full = (STEP, EDGE)
    panels = EDGE // STEP
    sub = lax.broadcasted_iota(jnp.int32, full, 0)
    lane = lax.broadcasted_iota(jnp.int32, full, 1)

    def spread(x, at):
        return [
            jnp.take_along_axis(
                x, jnp.full(full, at + i, jnp.int32), axis=1, mode="promise_in_bounds"
            )
            for i in range(STEP)
        ]

    rows = strips[0]
    for p in range(panels):
        at = p * STEP
        inside = (lane >= at) & (lane < at + STEP)
        swept = jnp.where(inside, jnp.where(lane == sub + at, -1.0, 0.0), rows)
        weights = spread(strips[p + 1], at) if p + 1 < panels else None
        solved = eliminate(swept, spread(rows, at))
        if weights is not None:
            terms = [w * jnp.broadcast_to(solved[k : k + 1], full) for k, w in enumerate(weights)]
            while len(terms) > 1:
                terms = [x + y for x, y in zip(terms[::2], terms[1::2])]
            rows = jnp.where(inside, 0.0, strips[p + 1]) - terms[0]
        change = fine(swept, solved, TURNED)
        if p < len(beside):
            beside[p]()
        strips = [
            rows
            if q == p + 1
            else (jnp.zeros(full, jnp.float32) if q == p else jnp.where(inside, 0.0, strips[q]))
            - change[q * STEP : (q + 1) * STEP]
            for q in range(panels)
        ]
    return jnp.concatenate(strips, axis=0)


def inverse_scale(count_ref):
    return 1.0 / (BLOCK * count_ref[0]).astype(jnp.float32)


def loading():
    return jnp.where(edge_iota(0) == edge_iota(1), LOADING, 0.0)


def minus_inverse(block, beside=()):
    return negative_inverse([block[q : q + STEP] for q in range(0, EDGE, STEP)], beside)


def corner_kernel(count_ref, own_ref, other_ref, minus_ref):
    both = own_ref[...] + other_ref[...]
    block = jnp.where(edge_iota(0) <= edge_iota(1), both, both.T)
    minus_ref[...] = minus_inverse(block * inverse_scale(count_ref) + loading())


def side_kernel(
    count_ref, own_corner, other_corner, own_ref, other_ref, steer_ref, minus_ref,
    made_ref, less_ref, next_ref,
):
    inv_scale = inverse_scale(count_ref)
    side = own_ref[...] + other_ref[...]
    near, far = side[:EDGE] * inv_scale, side[EDGE : 2 * EDGE] * inv_scale
    minus = minus_ref[...]
    r, c = edge_iota(0), edge_iota(1)
    both = own_corner[...] + other_corner[...]
    diag = side[2 * EDGE : 2 * EDGE + 1]
    block = jnp.where(r > c, both, jnp.where(r < c, both.T, diag)) * inv_scale + loading()
    close = -fine(minus, near)
    block = block - fine(near, close, TURNED)
    made_ref[:, :EDGE] = close
    right = steer_ref[pl.ds(0, EDGE), :].astype(jnp.float32)
    made = {}

    def solve(name, x, at):
        made[name] = -fine(minus, x)
        made_ref[:, at : at + x.shape[1]] = made[name]

    def take(i, lhs, name, at):
        less_ref[i, :, at : at + made[name].shape[1]] = fine(lhs, made[name], TURNED)

    next_ref[...] = minus_inverse(
        block,
        [
            lambda: solve("far", far, EDGE),
            lambda: solve("right", right, 2 * EDGE),
            lambda: take(0, near, "far", 0),
            lambda: take(1, far, "far", 0),
            lambda: take(0, near, "right", EDGE),
            lambda: take(1, far, "right", EDGE),
        ],
    )


def late_kernel(
    count_ref, own_late, other_late, own_side, other_side, steer_ref, made_ref, less_ref,
    minus_ref, out_ref,
):
    size, beams = steer_ref.shape
    parts = size // EDGE
    inv_scale = inverse_scale(count_ref)
    diag = own_side[pl.ds(2 * EDGE, 8), :] + other_side[pl.ds(2 * EDGE, 8), :]
    near, block = unpack_late(own_late[...] + other_late[...], diag[1:2])
    near = near * inv_scale - less_ref[0, :, :EDGE]
    block = block * inv_scale + loading() - less_ref[1, :, :EDGE]
    minus = minus_ref[...]
    step = -fine(minus, near)
    block = block - fine(near, step, TURNED)
    right = [
        steer_ref[pl.ds(i * EDGE, EDGE), :].astype(jnp.float32) - less_ref[i - 1, :, EDGE:]
        for i in (1, 2)
    ]
    made = made_ref[...]
    close, far, top = made[:, :EDGE], made[:, EDGE : 2 * EDGE], made[:, 2 * EDGE :]
    got = {}

    def middle():
        got["middle"] = -fine(minus, right[0])

    def last():
        got["last"] = right[1] - fine(near, got["middle"], TURNED)

    def base():
        got["base"] = jnp.concatenate([top - fine(close, got["middle"]), got["middle"]], axis=0)

    def turn():
        got["turn"] = jnp.concatenate([far - fine(close, step), step], axis=0)

    x = -fine(minus_inverse(block, [middle, last, base, turn]), got["last"])
    base, turn = got["base"], got["turn"]
    found = jnp.concatenate([base - fine(turn, x), x], axis=0)
    response = jnp.sum(steer_ref[...].astype(jnp.float32) * found, axis=0, keepdims=True)
    out_ref[...] = (found * (1.0 / response)).astype(out_ref.dtype)


def make_weights(count, own, other, steering):
    size, beams = steering.shape
    smem = pl.BlockSpec(memory_space=pltpu.SMEM)
    vmem = pl.BlockSpec(memory_space=pltpu.VMEM)
    wide = EDGE + beams
    square = jax.ShapeDtypeStruct((EDGE, EDGE), jnp.float32)

    def call(kernel, out_shape, *args):
        return pl.pallas_call(
            kernel,
            out_shape=out_shape,
            in_specs=[smem] + [vmem] * len(args),
            out_specs=jax.tree.map(lambda _: vmem, out_shape),
            compiler_params=pltpu.CompilerParams(vmem_limit_bytes=VMEM_BYTES),
            cost_estimate=pl.CostEstimate(flops=10**9, bytes_accessed=10**6, transcendentals=0),
        )(count, *args)

    corner = call(corner_kernel, square, own[0], other[0])
    made, less, second = call(
        side_kernel,
        [
            jax.ShapeDtypeStruct((EDGE, EDGE + wide), jnp.float32),
            jax.ShapeDtypeStruct((2, EDGE, wide), jnp.float32),
            square,
        ],
        own[0], other[0], own[1], other[1], steering, corner,
    )
    return call(
        late_kernel,
        jax.ShapeDtypeStruct((size, beams), jnp.bfloat16),
        own[2], other[2], own[1], other[1], steering, made, less, second,
    )


def split_kernel(which_ref, x_ref, out_ref):
    out_ref[:, 0] = x_ref[0]


def split(which, x):
    halves, group, rows, wide = x.shape
    chunks = 4
    return pl.pallas_call(
        split_kernel,
        out_shape=jax.ShapeDtypeStruct((group, halves, rows, wide), x.dtype),
        grid_spec=pltpu.PrefetchScalarGridSpec(
            num_scalar_prefetch=1,
            grid=(halves, chunks),
            in_specs=[
                pl.BlockSpec(
                    (1, group // chunks, rows, wide), lambda s, i, which: (which[s], i, 0, 0)
                )
            ],
            out_specs=pl.BlockSpec(
                (group // chunks, 1, rows, wide), lambda s, i, which: (i, s, 0, 0)
            ),
        ),
        compiler_params=pltpu.CompilerParams(vmem_limit_bytes=SPLIT_BYTES),
        cost_estimate=pl.CostEstimate(flops=0, bytes_accessed=2 * x.size, transcendentals=0),
    )(which, x)


def body(halves, snapshots, steering, train_list, train_count):
    bin_total, gate_rows, channels = snapshots.shape
    half = lax.axis_index("half").astype(jnp.int32)
    group = bin_total // halves
    order, base = jnp.stack([half, 1 - half]), half[None] * group
    peers = [(0, 1), (1, 0)]

    def exchange(x):
        return lax.all_to_all(x, INNER, split_axis=0, concat_axis=0, tiled=True)

    other_list = lax.ppermute(train_list, "half", peers)
    other_count = lax.ppermute(train_count, "half", peers)
    outgoing = split(order, snapshots.reshape(halves, group, gate_rows, channels))
    outgoing, other_list, other_count, base = lax.optimization_barrier(
        (outgoing, other_list, other_count, base)
    )
    blocks = exchange(outgoing)

    other_gram = partial_gram(1, base, other_list, other_count, blocks)
    arrived = [lax.ppermute(x, "half", peers) for x in other_gram]
    own_gram = partial_gram(0, base, train_list, train_count, blocks)
    weights = make_weights(train_count, own_gram, arrived, steering[0])
    other_weights = lax.ppermute(weights, "half", peers)

    def beams(x, w):
        made = jnp.einsum("ngd,de->nge", x, w, preferred_element_type=jnp.float32)
        return made.astype(jnp.bfloat16)

    made = jnp.stack([beams(blocks[:, 0], weights), beams(blocks[:, 1], other_weights)], axis=1)
    made, here, there = lax.optimization_barrier((made, half, 1 - half))
    out = jnp.moveaxis(exchange(made), 1, 0)
    sets = [
        lax.dynamic_index_in_dim(out, at, 0, keepdims=False, allow_negative_indices=False)
        for at in (here, there)
    ]
    return jnp.concatenate(sets, axis=0)


def solution(mesh):
    ranges, dopplers = mesh.devices.shape
    halves = 2
    cut = Mesh(mesh.devices.reshape(halves, ranges // halves, dopplers), EVERY)

    def run(*args):
        return body(halves, *args)

    return jax.shard_map(
        run,
        mesh=cut,
        in_specs=(P(None, EVERY, None), P(EVERY, None, None), P(EVERY, None), P(EVERY)),
        out_specs=P(None, EVERY, None),
        check_vma=False,
    )
```

```python
import functools

import jax
import jax.numpy as jnp
from jax import lax
from jax.experimental import pallas as pl
from jax.experimental.pallas import tpu as pltpu
from jax.sharding import Mesh
from jax.sharding import PartitionSpec as P

BLOCK = 128
LOADING = 0.1
EDGE = 128
STEP = 16
PACKED = (EDGE, 2 * EDGE + 8, EDGE + EDGE // 2)
INNER = ("inner", "doppler")
EVERY = ("half",) + INNER
VMEM_BYTES = 16 * 1024 * 1024
TURNED = (((0,), (0,)), ((), ()))
SPLIT_BYTES = 16 * 1024 * 1024


def edge_iota(dim, rows=EDGE):
    return lax.broadcasted_iota(jnp.int32, (rows, EDGE), dim)


def gram_kernel(which, base_ref, list_ref, count_ref, blocks_ref, corner_ref, side_ref, late_ref, chosen):
    group, _, rows, size = blocks_ref.shape
    for p in range(list_ref.shape[1]):
        chosen[list_ref[0, p]] = (p < count_ref[0]).astype(jnp.int32)
    every = [blocks_ref[n, which] for n in range(group)]
    kept = [
        jnp.where(chosen[base_ref[0] + n] > 0, x, jnp.zeros_like(x)) for n, x in enumerate(every)
    ]
    every = jnp.concatenate(every, axis=0)
    kept = jnp.concatenate(kept, axis=0)

    def strip(i):
        return lax.dot_general(
            kept[:, i * EDGE : (i + 1) * EDGE], every[:, i * EDGE :], (((0,), (0,)), ((), ())),
            preferred_element_type=jnp.float32,
        )

    half = EDGE // 2
    r, c = edge_iota(0), edge_iota(1)
    zero, one, two = strip(0), strip(1), strip(2)
    corner_ref[...] = jnp.where(r <= c, zero[:, :EDGE], one[:, :EDGE])
    side_ref[pl.ds(0, EDGE), :] = zero[:, EDGE : 2 * EDGE]
    side_ref[pl.ds(EDGE, EDGE), :] = zero[:, 2 * EDGE :]
    late_ref[pl.ds(0, EDGE), :] = one[:, EDGE:]
    low = pltpu.roll(two[half:], half, axis=1)
    rh, ch = r[:half], c[:half]
    late_ref[pl.ds(EDGE, half), :] = jnp.where((ch < half) & (rh > ch), low, two[:half])
    first = jnp.sum(jnp.where(r == c, one[:, :EDGE], 0.0), axis=0, keepdims=True)
    second = jnp.sum(jnp.where(rh == ch, low, 0.0), axis=0, keepdims=True)
    s = edge_iota(0, 8)
    side_ref[pl.ds(2 * EDGE, 8), :] = jnp.where(s == 0, first, jnp.where(s == 1, second, 0.0))


def partial_gram(which, base, lists, counts, blocks):
    group, _, rows, size = blocks.shape
    smem = pl.BlockSpec(memory_space=pltpu.SMEM)
    vmem = pl.BlockSpec(memory_space=pltpu.VMEM)
    return pl.pallas_call(
        functools.partial(gram_kernel, which),
        out_shape=[jax.ShapeDtypeStruct((n, EDGE), jnp.float32) for n in PACKED],
        in_specs=[smem, smem, smem, vmem],
        out_specs=[vmem] * len(PACKED),
        scratch_shapes=[pltpu.SMEM((lists.shape[1],), jnp.int32)],
        compiler_params=pltpu.CompilerParams(vmem_limit_bytes=3 * VMEM_BYTES),
        cost_estimate=pl.CostEstimate(
            flops=2 * group * rows * size * size,
            bytes_accessed=2 * group * rows * size,
            transcendentals=0,
        ),
    )(base, lists, counts, blocks)


def unpack_late(late, diag):
    half = EDGE // 2
    r, c = edge_iota(0, half), edge_iota(1, half)
    top = late[EDGE:]
    side = jnp.concatenate([top, jnp.zeros_like(top)], axis=0).T
    upper = jnp.where((c < half) & (r > c), side[:half], top)
    low = jnp.where(r > c, top, jnp.where(r < c, side[:half], diag))
    lower = jnp.where(c < half, side[half:], pltpu.roll(low, half, axis=1))
    return late[:EDGE], jnp.concatenate([upper, lower], axis=0)


def thirds(x):
    hi = x.astype(jnp.bfloat16)
    rest = x - hi.astype(jnp.float32)
    mid = rest.astype(jnp.bfloat16)
    low = (rest - mid.astype(jnp.float32)).astype(jnp.bfloat16)
    return hi, mid, low


def fine(a, b, dims=(((1,), (0,)), ((), ()))):
    ah, am, al = thirds(a)
    bh, bm, bl = thirds(b)
    left = jnp.concatenate([ah, ah, ah, am, am, al], axis=dims[0][0][0])
    right = jnp.concatenate([bh, bm, bl, bh, bm, bh], axis=dims[0][1][0])
    return lax.dot_general(left, right, dims, preferred_element_type=jnp.float32)


def spread(x, at):
    full = (STEP, EDGE)
    return [
        jnp.take_along_axis(x, jnp.full(full, at + i, jnp.int32), axis=1, mode="promise_in_bounds")
        for i in range(STEP)
    ]


def lower_inverse(block, beside=()):
    full = (STEP, EDGE)
    panels = EDGE // STEP
    sub = lax.broadcasted_iota(jnp.int32, full, 0)
    lane = lax.broadcasted_iota(jnp.int32, full, 1)

    def row(x, k):
        return jnp.broadcast_to(x[k : k + 1], full)

    strips = [block[q : q + STEP] for q in range(0, EDGE, STEP)]
    rows = strips[0]
    for p in range(panels):
        at = p * STEP
        inside = (lane >= at) & (lane < at + STEP)
        cols = spread(rows, at)
        ahead = spread(strips[p + 1], at) if p + 1 < panels else None
        rows = jnp.where(inside, jnp.where(lane == sub + at, 1.0, 0.0), rows)
        pivots = jnp.zeros(full, jnp.float32)
        terms = []
        for k in range(STEP):
            inv = 1.0 / row(cols[k], k)
            pivots = jnp.where(sub == k, cols[k], pivots)
            factor = jnp.where(sub > k, cols[k] * inv, 0.0)
            if ahead is not None:
                terms.append(ahead[k] * (row(rows, k) * inv))
            for i in range(k + 1, STEP):
                value = row(cols[i], k)
                cols[i] = cols[i] - factor * value
                if ahead is not None:
                    ahead[i] = ahead[i] - ahead[k] * (value * inv)
            rows = rows - factor * row(rows, k)
        made = rows * lax.rsqrt(pivots)
        if ahead is not None:
            while len(terms) > 1:
                terms = [x + y for x, y in zip(terms[::2], terms[1::2])]
            rows = jnp.where(inside, 0.0, strips[p + 1]) - terms[0]
            change = fine(made, made, TURNED)
        for call in beside[p : p + 1] if p + 1 < panels else beside[p:]:
            call()
        strips = [
            made
            if q == p
            else strips[q]
            if q < p
            else rows
            if q == p + 1
            else jnp.where(inside, 0.0, strips[q]) - change[q * STEP : (q + 1) * STEP]
            for q in range(panels)
        ]
    inverse = jnp.concatenate(strips, axis=0)
    return jnp.where(edge_iota(0) >= edge_iota(1), inverse, 0.0)


def inverse_scale(count_ref):
    return 1.0 / (BLOCK * count_ref[0]).astype(jnp.float32)


def loading():
    return jnp.where(edge_iota(0) == edge_iota(1), LOADING, 0.0)


def corner_kernel(count_ref, own_ref, other_ref, lower_ref):
    both = own_ref[...] + other_ref[...]
    block = jnp.where(edge_iota(0) <= edge_iota(1), both, both.T)
    lower_ref[...] = lower_inverse(block * inverse_scale(count_ref) + loading())


def side_kernel(
    count_ref, own_corner, other_corner, own_ref, other_ref, steer_ref, lower_ref,
    made_ref, less_ref, next_ref,
):
    inv_scale = inverse_scale(count_ref)
    side = own_ref[...] + other_ref[...]
    near, far = side[:EDGE] * inv_scale, side[EDGE : 2 * EDGE] * inv_scale
    lower = lower_ref[...]
    r, c = edge_iota(0), edge_iota(1)
    both = own_corner[...] + other_corner[...]
    diag = side[2 * EDGE : 2 * EDGE + 1]
    block = jnp.where(r > c, both, jnp.where(r < c, both.T, diag)) * inv_scale + loading()
    half = {"near": fine(lower, near)}
    block = block - fine(half["near"], half["near"], TURNED)
    right = steer_ref[pl.ds(0, EDGE), :].astype(jnp.float32)

    def forward(name, x):
        half[name] = fine(lower, x)

    def back(name, at):
        x = half[name]
        made_ref[:, at : at + x.shape[1]] = fine(lower, x, TURNED)

    def take(i, lhs, name, at):
        x = half[name]
        less_ref[i, :, at : at + x.shape[1]] = fine(half[lhs], x, TURNED)

    next_ref[...] = lower_inverse(
        block,
        [
            lambda: forward("far", far),
            lambda: forward("right", right),
            lambda: take(0, "near", "far", 0),
            lambda: take(1, "far", "far", 0),
            lambda: take(0, "near", "right", EDGE),
            lambda: take(1, "far", "right", EDGE),
            lambda: back("near", 0),
            lambda: back("far", EDGE),
            lambda: back("right", 2 * EDGE),
        ],
    )


def late_kernel(
    count_ref, own_late, other_late, own_side, other_side, steer_ref, made_ref, less_ref,
    lower_ref, out_ref,
):
    size, beams = steer_ref.shape
    inv_scale = inverse_scale(count_ref)
    diag = own_side[pl.ds(2 * EDGE, 8), :] + other_side[pl.ds(2 * EDGE, 8), :]
    near, block = unpack_late(own_late[...] + other_late[...], diag[1:2])
    near = near * inv_scale - less_ref[0, :, :EDGE]
    block = block * inv_scale + loading() - less_ref[1, :, :EDGE]
    lower = lower_ref[...]
    near = fine(lower, near)
    block = block - fine(near, near, TURNED)
    right = [
        steer_ref[pl.ds(i * EDGE, EDGE), :].astype(jnp.float32) - less_ref[i - 1, :, EDGE:]
        for i in (1, 2)
    ]
    made = made_ref[...]
    close, far, top = made[:, :EDGE], made[:, EDGE : 2 * EDGE], made[:, 2 * EDGE :]
    got = {}

    def forward():
        got["half"] = fine(lower, right[0])

    def last():
        got["last"] = right[1] - fine(near, got["half"], TURNED)

    def middle():
        got["middle"] = fine(lower, got["half"], TURNED)

    def step():
        got["step"] = fine(lower, near, TURNED)

    def base():
        got["base"] = jnp.concatenate([top - fine(close, got["middle"]), got["middle"]], axis=0)

    def turn():
        got["turn"] = jnp.concatenate([far - fine(close, got["step"]), got["step"]], axis=0)

    end = lower_inverse(block, [forward, last, middle, step, base, turn])
    x = fine(end, fine(end, got["last"]), TURNED)
    found = jnp.concatenate([got["base"] - fine(got["turn"], x), x], axis=0)
    response = jnp.sum(steer_ref[...].astype(jnp.float32) * found, axis=0, keepdims=True)
    out_ref[...] = (found * (1.0 / response)).astype(out_ref.dtype)


def make_weights(count, own, other, steering):
    size, beams = steering.shape
    smem = pl.BlockSpec(memory_space=pltpu.SMEM)
    vmem = pl.BlockSpec(memory_space=pltpu.VMEM)
    wide = EDGE + beams
    square = jax.ShapeDtypeStruct((EDGE, EDGE), jnp.float32)

    def call(kernel, out_shape, *args):
        return pl.pallas_call(
            kernel,
            out_shape=out_shape,
            in_specs=[smem] + [vmem] * len(args),
            out_specs=jax.tree.map(lambda _: vmem, out_shape),
            compiler_params=pltpu.CompilerParams(vmem_limit_bytes=VMEM_BYTES),
            cost_estimate=pl.CostEstimate(flops=10**9, bytes_accessed=10**6, transcendentals=0),
        )(count, *args)

    corner = call(corner_kernel, square, own[0], other[0])
    made, less, second = call(
        side_kernel,
        [
            jax.ShapeDtypeStruct((EDGE, EDGE + wide), jnp.float32),
            jax.ShapeDtypeStruct((2, EDGE, wide), jnp.float32),
            square,
        ],
        own[0], other[0], own[1], other[1], steering, corner,
    )
    return call(
        late_kernel,
        jax.ShapeDtypeStruct((size, beams), jnp.bfloat16),
        own[2], other[2], own[1], other[1], steering, made, less, second,
    )


def split_kernel(which_ref, x_ref, out_ref):
    out_ref[:, 0] = x_ref[0]


def split(which, x):
    halves, group, rows, wide = x.shape
    chunks = 4
    return pl.pallas_call(
        split_kernel,
        out_shape=jax.ShapeDtypeStruct((group, halves, rows, wide), x.dtype),
        grid_spec=pltpu.PrefetchScalarGridSpec(
            num_scalar_prefetch=1,
            grid=(halves, chunks),
            in_specs=[
                pl.BlockSpec(
                    (1, group // chunks, rows, wide), lambda s, i, which: (which[s], i, 0, 0)
                )
            ],
            out_specs=pl.BlockSpec(
                (group // chunks, 1, rows, wide), lambda s, i, which: (i, s, 0, 0)
            ),
        ),
        compiler_params=pltpu.CompilerParams(vmem_limit_bytes=SPLIT_BYTES),
        cost_estimate=pl.CostEstimate(flops=0, bytes_accessed=2 * x.size, transcendentals=0),
    )(which, x)


def body(halves, snapshots, steering, train_list, train_count):
    bin_total, gate_rows, channels = snapshots.shape
    half = lax.axis_index("half").astype(jnp.int32)
    group = bin_total // halves
    order, base = jnp.stack([half, 1 - half]), half[None] * group
    peers = [(0, 1), (1, 0)]

    def exchange(x):
        return lax.all_to_all(x, INNER, split_axis=0, concat_axis=0, tiled=True)

    other_list = lax.ppermute(train_list, "half", peers)
    other_count = lax.ppermute(train_count, "half", peers)
    outgoing = split(order, snapshots.reshape(halves, group, gate_rows, channels))
    outgoing, other_list, other_count, base = lax.optimization_barrier(
        (outgoing, other_list, other_count, base)
    )
    blocks = exchange(outgoing)

    other_gram = partial_gram(1, base, other_list, other_count, blocks)
    arrived = [lax.ppermute(x, "half", peers) for x in other_gram]
    own_gram = partial_gram(0, base, train_list, train_count, blocks)
    weights = make_weights(train_count, own_gram, arrived, steering[0])
    other_weights = lax.ppermute(weights, "half", peers)

    def beams(x, w):
        made = jnp.einsum("ngd,de->nge", x, w, preferred_element_type=jnp.float32)
        return made.astype(jnp.bfloat16)

    made = jnp.stack([beams(blocks[:, 0], weights), beams(blocks[:, 1], other_weights)], axis=1)
    made, here, there = lax.optimization_barrier((made, half, 1 - half))
    out = jnp.moveaxis(exchange(made), 1, 0)
    sets = [
        lax.dynamic_index_in_dim(out, at, 0, keepdims=False, allow_negative_indices=False)
        for at in (here, there)
    ]
    return jnp.concatenate(sets, axis=0)


def solution(mesh):
    ranges, dopplers = mesh.devices.shape
    halves = 2
    cut = Mesh(mesh.devices.reshape(halves, ranges // halves, dopplers), EVERY)

    def run(*args):
        return body(halves, *args)

    return jax.shard_map(
        run,
        mesh=cut,
        in_specs=(P(None, EVERY, None), P(EVERY, None, None), P(EVERY, None), P(EVERY)),
        out_specs=P(None, EVERY, None),
        check_vma=False,
    )
```

```python
import functools

import jax
import jax.numpy as jnp
from jax import lax
from jax.experimental import pallas as pl
from jax.experimental.pallas import tpu as pltpu
from jax.sharding import Mesh
from jax.sharding import PartitionSpec as P

BLOCK = 128
LOADING = 0.1
EDGE = 128
STEP = 16
PACKED = (EDGE, 2 * EDGE + 8, EDGE + EDGE // 2)
INNER = ("inner", "doppler")
EVERY = ("half",) + INNER
VMEM_BYTES = 16 * 1024 * 1024
TURNED = (((0,), (0,)), ((), ()))


def edge_iota(dim, rows=EDGE):
    return lax.broadcasted_iota(jnp.int32, (rows, EDGE), dim)


def gram_kernel(which, base_ref, list_ref, count_ref, blocks_ref, corner_ref, side_ref, late_ref, chosen):
    group, _, rows, size = blocks_ref.shape
    for p in range(list_ref.shape[1]):
        chosen[list_ref[0, p]] = (p < count_ref[0]).astype(jnp.int32)
    every = [blocks_ref[n, which] for n in range(group)]
    kept = [
        jnp.where(chosen[base_ref[0] + n] > 0, x, jnp.zeros_like(x)) for n, x in enumerate(every)
    ]
    every = jnp.concatenate(every, axis=0)
    kept = jnp.concatenate(kept, axis=0)

    def strip(i):
        return lax.dot_general(
            kept[:, i * EDGE : (i + 1) * EDGE], every[:, i * EDGE :], (((0,), (0,)), ((), ())),
            preferred_element_type=jnp.float32,
        )

    half = EDGE // 2
    r, c = edge_iota(0), edge_iota(1)
    zero, one, two = strip(0), strip(1), strip(2)
    corner_ref[...] = jnp.where(r <= c, zero[:, :EDGE], one[:, :EDGE])
    side_ref[pl.ds(0, EDGE), :] = zero[:, EDGE : 2 * EDGE]
    side_ref[pl.ds(EDGE, EDGE), :] = zero[:, 2 * EDGE :]
    late_ref[pl.ds(0, EDGE), :] = one[:, EDGE:]
    low = pltpu.roll(two[half:], half, axis=1)
    rh, ch = r[:half], c[:half]
    late_ref[pl.ds(EDGE, half), :] = jnp.where((ch < half) & (rh > ch), low, two[:half])
    first = jnp.sum(jnp.where(r == c, one[:, :EDGE], 0.0), axis=0, keepdims=True)
    second = jnp.sum(jnp.where(rh == ch, low, 0.0), axis=0, keepdims=True)
    s = edge_iota(0, 8)
    side_ref[pl.ds(2 * EDGE, 8), :] = jnp.where(s == 0, first, jnp.where(s == 1, second, 0.0))


def partial_gram(which, base, lists, counts, blocks):
    group, _, rows, size = blocks.shape
    smem = pl.BlockSpec(memory_space=pltpu.SMEM)
    vmem = pl.BlockSpec(memory_space=pltpu.VMEM)
    return pl.pallas_call(
        functools.partial(gram_kernel, which),
        out_shape=[jax.ShapeDtypeStruct((n, EDGE), jnp.float32) for n in PACKED],
        in_specs=[smem, smem, smem, vmem],
        out_specs=[vmem] * len(PACKED),
        scratch_shapes=[pltpu.SMEM((lists.shape[1],), jnp.int32)],
        compiler_params=pltpu.CompilerParams(vmem_limit_bytes=3 * VMEM_BYTES),
        cost_estimate=pl.CostEstimate(
            flops=2 * group * rows * size * size,
            bytes_accessed=2 * group * rows * size,
            transcendentals=0,
        ),
    )(base, lists, counts, blocks)


def unpack_late(late, diag):
    half = EDGE // 2
    r, c = edge_iota(0, half), edge_iota(1, half)
    top = late[EDGE:]
    side = jnp.concatenate([top, jnp.zeros_like(top)], axis=0).T
    upper = jnp.where((c < half) & (r > c), side[:half], top)
    low = jnp.where(r > c, top, jnp.where(r < c, side[:half], diag))
    lower = jnp.where(c < half, side[half:], pltpu.roll(low, half, axis=1))
    return late[:EDGE], jnp.concatenate([upper, lower], axis=0)


def thirds(x):
    hi = x.astype(jnp.bfloat16)
    rest = x - hi.astype(jnp.float32)
    mid = rest.astype(jnp.bfloat16)
    low = (rest - mid.astype(jnp.float32)).astype(jnp.bfloat16)
    return hi, mid, low


def fine(a, b, dims=(((1,), (0,)), ((), ()))):
    ah, am, al = thirds(a)
    bh, bm, bl = thirds(b)
    left = jnp.concatenate([ah, ah, ah, am, am, al], axis=dims[0][0][0])
    right = jnp.concatenate([bh, bm, bl, bh, bm, bh], axis=dims[0][1][0])
    return lax.dot_general(left, right, dims, preferred_element_type=jnp.float32)


def spread(x, at):
    full = (STEP, EDGE)
    return [
        jnp.take_along_axis(x, jnp.full(full, at + i, jnp.int32), axis=1, mode="promise_in_bounds")
        for i in range(STEP)
    ]


def lower_inverse(block, beside=()):
    full = (STEP, EDGE)
    panels = EDGE // STEP
    sub = lax.broadcasted_iota(jnp.int32, full, 0)
    lane = lax.broadcasted_iota(jnp.int32, full, 1)

    piece = lax.broadcasted_iota(jnp.int32, (8, EDGE), 0)

    def row(x, k):
        return jnp.broadcast_to(x[k : k + 1], (8, EDGE))

    def cut(x):
        return [x[q : q + 8] for q in range(0, STEP, 8)]

    strips = [block[q : q + STEP] for q in range(0, EDGE, STEP)]
    rows = strips[0]
    for p in range(panels):
        at = p * STEP
        inside = (lane >= at) & (lane < at + STEP)
        cols = spread(rows, at)
        ahead = spread(strips[p + 1], at) if p + 1 < panels else None
        rows = jnp.where(inside, jnp.where(lane == sub + at, 1.0, 0.0), rows)
        cols = [cut(x) for x in cols]
        done = cut(rows)
        pivots = cut(jnp.zeros(full, jnp.float32))
        terms = []
        for k in range(STEP):
            own, at_k = divmod(k, 8)
            inv = 1.0 / row(cols[k][own], at_k)
            pivots[own] = jnp.where(piece == at_k, cols[k][own], pivots[own])
            factors = {own: jnp.where(piece > at_k, cols[k][own] * inv, 0.0)}
            for q in range(own + 1, STEP // 8):
                factors[q] = cols[k][q] * inv
            used = row(done[own], at_k)
            if ahead is not None:
                terms.append(ahead[k] * jnp.concatenate([used * inv] * (STEP // 8), axis=0))
            for i in range(k + 1, STEP):
                value = row(cols[i][own], at_k)
                for q, factor in factors.items():
                    cols[i][q] = cols[i][q] - factor * value
                if ahead is not None:
                    scaled = jnp.concatenate([value * inv] * (STEP // 8), axis=0)
                    ahead[i] = ahead[i] - ahead[k] * scaled
            for q, factor in factors.items():
                done[q] = done[q] - factor * used
        rows, pivots = jnp.concatenate(done, axis=0), jnp.concatenate(pivots, axis=0)
        made = rows * lax.rsqrt(pivots)
        if ahead is not None:
            while len(terms) > 1:
                terms = [x + y for x, y in zip(terms[::2], terms[1::2])]
            rows = jnp.where(inside, 0.0, strips[p + 1]) - terms[0]
            change = fine(made, made, TURNED)
        for call in beside[p : p + 1] if p + 1 < panels else beside[p:]:
            call()
        strips = [
            made
            if q == p
            else strips[q]
            if q < p
            else rows
            if q == p + 1
            else jnp.where(inside, 0.0, strips[q]) - change[q * STEP : (q + 1) * STEP]
            for q in range(panels)
        ]
    inverse = jnp.concatenate(strips, axis=0)
    return jnp.where(edge_iota(0) >= edge_iota(1), inverse, 0.0)


def inverse_scale(count_ref):
    return 1.0 / (BLOCK * count_ref[0]).astype(jnp.float32)


def loading():
    return jnp.where(edge_iota(0) == edge_iota(1), LOADING, 0.0)


def corner_kernel(count_ref, own_ref, other_ref, lower_ref):
    both = own_ref[...] + other_ref[...]
    block = jnp.where(edge_iota(0) <= edge_iota(1), both, both.T)
    lower_ref[...] = lower_inverse(block * inverse_scale(count_ref) + loading())


def side_kernel(
    count_ref, own_corner, other_corner, own_ref, other_ref, steer_ref, lower_ref,
    made_ref, less_ref, next_ref,
):
    inv_scale = inverse_scale(count_ref)
    side = own_ref[...] + other_ref[...]
    near, far = side[:EDGE] * inv_scale, side[EDGE : 2 * EDGE] * inv_scale
    lower = lower_ref[...]
    r, c = edge_iota(0), edge_iota(1)
    both = own_corner[...] + other_corner[...]
    diag = side[2 * EDGE : 2 * EDGE + 1]
    block = jnp.where(r > c, both, jnp.where(r < c, both.T, diag)) * inv_scale + loading()
    half = {"near": fine(lower, near)}
    block = block - fine(half["near"], half["near"], TURNED)
    right = steer_ref[pl.ds(0, EDGE), :].astype(jnp.float32)

    def forward(name, x):
        half[name] = fine(lower, x)

    def back(name, at):
        x = half[name]
        made_ref[:, at : at + x.shape[1]] = fine(lower, x, TURNED)

    def take(i, lhs, name, at):
        x = half[name]
        less_ref[i, :, at : at + x.shape[1]] = fine(half[lhs], x, TURNED)

    next_ref[...] = lower_inverse(
        block,
        [
            lambda: forward("far", far),
            lambda: forward("right", right),
            lambda: take(0, "near", "far", 0),
            lambda: take(1, "far", "far", 0),
            lambda: take(0, "near", "right", EDGE),
            lambda: take(1, "far", "right", EDGE),
            lambda: back("near", 0),
            lambda: back("far", EDGE),
            lambda: back("right", 2 * EDGE),
        ],
    )


def late_kernel(
    count_ref, own_late, other_late, own_side, other_side, steer_ref, made_ref, less_ref,
    lower_ref, out_ref,
):
    size, beams = steer_ref.shape
    inv_scale = inverse_scale(count_ref)
    diag = own_side[pl.ds(2 * EDGE, 8), :] + other_side[pl.ds(2 * EDGE, 8), :]
    near, block = unpack_late(own_late[...] + other_late[...], diag[1:2])
    near = near * inv_scale - less_ref[0, :, :EDGE]
    block = block * inv_scale + loading() - less_ref[1, :, :EDGE]
    lower = lower_ref[...]
    near = fine(lower, near)
    block = block - fine(near, near, TURNED)
    right = [
        steer_ref[pl.ds(i * EDGE, EDGE), :].astype(jnp.float32) - less_ref[i - 1, :, EDGE:]
        for i in (1, 2)
    ]
    made = made_ref[...]
    close, far, top = made[:, :EDGE], made[:, EDGE : 2 * EDGE], made[:, 2 * EDGE :]
    got = {}

    def forward():
        got["half"] = fine(lower, right[0])

    def last():
        got["last"] = right[1] - fine(near, got["half"], TURNED)

    def middle():
        got["middle"] = fine(lower, got["half"], TURNED)

    def step():
        got["step"] = fine(lower, near, TURNED)

    def base():
        got["base"] = jnp.concatenate([top - fine(close, got["middle"]), got["middle"]], axis=0)

    def turn():
        got["turn"] = jnp.concatenate([far - fine(close, got["step"]), got["step"]], axis=0)

    end = lower_inverse(block, [forward, last, middle, step, base, turn])
    x = fine(end, fine(end, got["last"]), TURNED)
    found = jnp.concatenate([got["base"] - fine(got["turn"], x), x], axis=0)
    response = jnp.sum(steer_ref[...].astype(jnp.float32) * found, axis=0, keepdims=True)
    out_ref[...] = (found * (1.0 / response)).astype(out_ref.dtype)


def make_weights(count, own, other, steering):
    size, beams = steering.shape
    smem = pl.BlockSpec(memory_space=pltpu.SMEM)
    vmem = pl.BlockSpec(memory_space=pltpu.VMEM)
    wide = EDGE + beams
    square = jax.ShapeDtypeStruct((EDGE, EDGE), jnp.float32)

    def call(kernel, out_shape, *args):
        return pl.pallas_call(
            kernel,
            out_shape=out_shape,
            in_specs=[smem] + [vmem] * len(args),
            out_specs=jax.tree.map(lambda _: vmem, out_shape),
            compiler_params=pltpu.CompilerParams(vmem_limit_bytes=VMEM_BYTES),
            cost_estimate=pl.CostEstimate(flops=10**9, bytes_accessed=10**6, transcendentals=0),
        )(count, *args)

    corner = call(corner_kernel, square, own[0], other[0])
    made, less, second = call(
        side_kernel,
        [
            jax.ShapeDtypeStruct((EDGE, EDGE + wide), jnp.float32),
            jax.ShapeDtypeStruct((2, EDGE, wide), jnp.float32),
            square,
        ],
        own[0], other[0], own[1], other[1], steering, corner,
    )
    return call(
        late_kernel,
        jax.ShapeDtypeStruct((size, beams), jnp.bfloat16),
        own[2], other[2], own[1], other[1], steering, made, less, second,
    )


def split_kernel(which_ref, x_ref, out_ref, sems):
    halves, group = x_ref.shape[:2]
    chunk = group // 4
    copies = []
    for s in range(halves):
        for i in range(4):
            part = pl.ds(i * chunk, chunk)
            copies.append(
                pltpu.make_async_copy(
                    x_ref.at[which_ref[s], part], out_ref.at[part, s], sems.at[s, i]
                )
            )
    for copy in copies:
        copy.start()
    for copy in copies:
        copy.wait()


def split(which, x):
    halves, group, rows, wide = x.shape
    return pl.pallas_call(
        split_kernel,
        out_shape=jax.ShapeDtypeStruct((group, halves, rows, wide), x.dtype),
        in_specs=[pl.BlockSpec(memory_space=pltpu.SMEM), pl.BlockSpec(memory_space=pltpu.HBM)],
        out_specs=pl.BlockSpec(memory_space=pltpu.VMEM),
        scratch_shapes=[pltpu.SemaphoreType.DMA((halves, 4))],
        compiler_params=pltpu.CompilerParams(vmem_limit_bytes=2 * VMEM_BYTES),
        cost_estimate=pl.CostEstimate(flops=0, bytes_accessed=2 * x.size, transcendentals=0),
    )(which, x)


def body(halves, snapshots, steering, train_list, train_count):
    bin_total, gate_rows, channels = snapshots.shape
    half = lax.axis_index("half").astype(jnp.int32)
    group = bin_total // halves
    order, base = jnp.stack([half, 1 - half]), half[None] * group
    peers = [(0, 1), (1, 0)]

    def exchange(x):
        return lax.all_to_all(x, INNER, split_axis=0, concat_axis=0, tiled=True)

    other_list = lax.ppermute(train_list, "half", peers)
    other_count = lax.ppermute(train_count, "half", peers)
    outgoing = split(order, snapshots.reshape(halves, group, gate_rows, channels))
    outgoing, other_list, other_count, base = lax.optimization_barrier(
        (outgoing, other_list, other_count, base)
    )
    blocks = exchange(outgoing)

    other_gram = partial_gram(1, base, other_list, other_count, blocks)
    arrived = [lax.ppermute(x, "half", peers) for x in other_gram]
    own_gram = partial_gram(0, base, train_list, train_count, blocks)
    weights = make_weights(train_count, own_gram, arrived, steering[0])
    other_weights = lax.ppermute(weights, "half", peers)

    def beams(x, w):
        made = jnp.einsum("ngd,de->nge", x, w, preferred_element_type=jnp.float32)
        return made.astype(jnp.bfloat16)

    made = jnp.stack([beams(blocks[:, 0], weights), beams(blocks[:, 1], other_weights)], axis=1)
    made, here, there = lax.optimization_barrier((made, half, 1 - half))
    out = jnp.moveaxis(exchange(made), 1, 0)
    sets = [
        lax.dynamic_index_in_dim(out, at, 0, keepdims=False, allow_negative_indices=False)
        for at in (here, there)
    ]
    return jnp.concatenate(sets, axis=0)


def solution(mesh):
    ranges, dopplers = mesh.devices.shape
    halves = 2
    cut = Mesh(mesh.devices.reshape(halves, ranges // halves, dopplers), EVERY)

    def run(*args):
        return body(halves, *args)

    return jax.shard_map(
        run,
        mesh=cut,
        in_specs=(P(None, EVERY, None), P(EVERY, None, None), P(EVERY, None), P(EVERY)),
        out_specs=P(None, EVERY, None),
        check_vma=False,
    )
```

```python
import functools

import jax
import jax.numpy as jnp
from jax import lax
from jax.experimental import pallas as pl
from jax.experimental.pallas import tpu as pltpu
from jax.sharding import Mesh
from jax.sharding import PartitionSpec as P

BLOCK = 128
LOADING = 0.1
EDGE = 128
STEP = 16
PACKED = (EDGE, 2 * EDGE + 8, EDGE + EDGE // 2)
INNER = ("inner", "doppler")
EVERY = ("half",) + INNER
VMEM_BYTES = 16 * 1024 * 1024
TURNED = (((0,), (0,)), ((), ()))


def edge_iota(dim, rows=EDGE):
    return lax.broadcasted_iota(jnp.int32, (rows, EDGE), dim)


def gram_kernel(which, base_ref, list_ref, count_ref, blocks_ref, corner_ref, side_ref, late_ref, chosen):
    group, _, rows, size = blocks_ref.shape
    for p in range(list_ref.shape[1]):
        chosen[list_ref[0, p]] = (p < count_ref[0]).astype(jnp.int32)
    every = [blocks_ref[n, which] for n in range(group)]
    kept = [
        jnp.where(chosen[base_ref[0] + n] > 0, x, jnp.zeros_like(x)) for n, x in enumerate(every)
    ]
    every = jnp.concatenate(every, axis=0)
    kept = jnp.concatenate(kept, axis=0)

    def strip(i):
        return lax.dot_general(
            kept[:, i * EDGE : (i + 1) * EDGE], every[:, i * EDGE :], (((0,), (0,)), ((), ())),
            preferred_element_type=jnp.float32,
        )

    half = EDGE // 2
    r, c = edge_iota(0), edge_iota(1)
    zero, one, two = strip(0), strip(1), strip(2)
    corner_ref[...] = jnp.where(r <= c, zero[:, :EDGE], one[:, :EDGE])
    side_ref[pl.ds(0, EDGE), :] = zero[:, EDGE : 2 * EDGE]
    side_ref[pl.ds(EDGE, EDGE), :] = zero[:, 2 * EDGE :]
    late_ref[pl.ds(0, EDGE), :] = one[:, EDGE:]
    low = pltpu.roll(two[half:], half, axis=1)
    rh, ch = r[:half], c[:half]
    late_ref[pl.ds(EDGE, half), :] = jnp.where((ch < half) & (rh > ch), low, two[:half])
    first = jnp.sum(jnp.where(r == c, one[:, :EDGE], 0.0), axis=0, keepdims=True)
    second = jnp.sum(jnp.where(rh == ch, low, 0.0), axis=0, keepdims=True)
    s = edge_iota(0, 8)
    side_ref[pl.ds(2 * EDGE, 8), :] = jnp.where(s == 0, first, jnp.where(s == 1, second, 0.0))


def partial_gram(which, base, lists, counts, blocks):
    group, _, rows, size = blocks.shape
    smem = pl.BlockSpec(memory_space=pltpu.SMEM)
    vmem = pl.BlockSpec(memory_space=pltpu.VMEM)
    return pl.pallas_call(
        functools.partial(gram_kernel, which),
        out_shape=[jax.ShapeDtypeStruct((n, EDGE), jnp.float32) for n in PACKED],
        in_specs=[smem, smem, smem, vmem],
        out_specs=[vmem] * len(PACKED),
        scratch_shapes=[pltpu.SMEM((lists.shape[1],), jnp.int32)],
        compiler_params=pltpu.CompilerParams(vmem_limit_bytes=3 * VMEM_BYTES),
        cost_estimate=pl.CostEstimate(
            flops=2 * group * rows * size * size,
            bytes_accessed=2 * group * rows * size,
            transcendentals=0,
        ),
    )(base, lists, counts, blocks)


def unpack_late(late, diag):
    half = EDGE // 2
    r, c = edge_iota(0, half), edge_iota(1, half)
    top = late[EDGE:]
    side = jnp.concatenate([top, jnp.zeros_like(top)], axis=0).T
    upper = jnp.where((c < half) & (r > c), side[:half], top)
    low = jnp.where(r > c, top, jnp.where(r < c, side[:half], diag))
    lower = jnp.where(c < half, side[half:], pltpu.roll(low, half, axis=1))
    return late[:EDGE], jnp.concatenate([upper, lower], axis=0)


def thirds(x):
    hi = x.astype(jnp.bfloat16)
    rest = x - hi.astype(jnp.float32)
    mid = rest.astype(jnp.bfloat16)
    low = (rest - mid.astype(jnp.float32)).astype(jnp.bfloat16)
    return hi, mid, low


def fine(a, b, dims=(((1,), (0,)), ((), ()))):
    ah, am, al = thirds(a)
    bh, bm, bl = thirds(b)
    left = jnp.concatenate([ah, ah, ah, am, am, al], axis=dims[0][0][0])
    right = jnp.concatenate([bh, bm, bl, bh, bm, bh], axis=dims[0][1][0])
    return lax.dot_general(left, right, dims, preferred_element_type=jnp.float32)


def spread(x, at):
    full = (STEP, EDGE)
    return [
        jnp.take_along_axis(x, jnp.full(full, at + i, jnp.int32), axis=1, mode="promise_in_bounds")
        for i in range(STEP)
    ]


def lower_inverse(block, beside=()):
    full = (STEP, EDGE)
    panels = EDGE // STEP
    sub = lax.broadcasted_iota(jnp.int32, full, 0)
    lane = lax.broadcasted_iota(jnp.int32, full, 1)

    piece = lax.broadcasted_iota(jnp.int32, (8, EDGE), 0)

    def row(x, k):
        return jnp.broadcast_to(x[k : k + 1], (8, EDGE))

    def cut(x):
        return [x[q : q + 8] for q in range(0, STEP, 8)]

    strips = [block[q : q + STEP] for q in range(0, EDGE, STEP)]
    rows = strips[0]
    for p in range(panels):
        at = p * STEP
        inside = (lane >= at) & (lane < at + STEP)
        cols = spread(rows, at)
        ahead = spread(strips[p + 1], at) if p + 1 < panels else None
        rows = jnp.where(inside, jnp.where(lane == sub + at, 1.0, 0.0), rows)
        cols = [cut(x) for x in cols]
        done = cut(rows)
        pivots = cut(jnp.zeros(full, jnp.float32))
        terms = []
        for k in range(STEP):
            own, at_k = divmod(k, 8)
            inv = 1.0 / row(cols[k][own], at_k)
            pivots[own] = jnp.where(piece == at_k, cols[k][own], pivots[own])
            factors = {own: jnp.where(piece > at_k, cols[k][own] * inv, 0.0)}
            for q in range(own + 1, STEP // 8):
                factors[q] = cols[k][q] * inv
            used = row(done[own], at_k)
            if ahead is not None:
                terms.append(ahead[k] * jnp.concatenate([used * inv] * (STEP // 8), axis=0))
            for i in range(k + 1, STEP):
                value = row(cols[i][own], at_k)
                for q, factor in factors.items():
                    cols[i][q] = cols[i][q] - factor * value
                if ahead is not None:
                    scaled = jnp.concatenate([value * inv] * (STEP // 8), axis=0)
                    ahead[i] = ahead[i] - ahead[k] * scaled
            for q, factor in factors.items():
                done[q] = done[q] - factor * used
        rows, pivots = jnp.concatenate(done, axis=0), jnp.concatenate(pivots, axis=0)
        made = rows * lax.rsqrt(pivots)
        if ahead is not None:
            while len(terms) > 1:
                terms = [x + y for x, y in zip(terms[::2], terms[1::2])]
            rows = jnp.where(inside, 0.0, strips[p + 1]) - terms[0]
            change = fine(made, made, TURNED)
        for call in beside[p : p + 1] if p + 1 < panels else beside[p:]:
            call()
        strips = [
            made
            if q == p
            else strips[q]
            if q < p
            else rows
            if q == p + 1
            else jnp.where(inside, 0.0, strips[q]) - change[q * STEP : (q + 1) * STEP]
            for q in range(panels)
        ]
    inverse = jnp.concatenate(strips, axis=0)
    return jnp.where(edge_iota(0) >= edge_iota(1), inverse, 0.0)


def inverse_scale(count_ref):
    return 1.0 / (BLOCK * count_ref[0]).astype(jnp.float32)


def loading():
    return jnp.where(edge_iota(0) == edge_iota(1), LOADING, 0.0)


def corner_kernel(count_ref, own_ref, other_ref, lower_ref):
    both = own_ref[...] + other_ref[...]
    block = jnp.where(edge_iota(0) <= edge_iota(1), both, both.T)
    lower_ref[...] = lower_inverse(block * inverse_scale(count_ref) + loading())


def side_kernel(
    count_ref, own_corner, other_corner, own_ref, other_ref, steer_ref, lower_ref,
    made_ref, less_ref, next_ref,
):
    inv_scale = inverse_scale(count_ref)
    side = own_ref[...] + other_ref[...]
    near, far = side[:EDGE] * inv_scale, side[EDGE : 2 * EDGE] * inv_scale
    lower = lower_ref[...]
    r, c = edge_iota(0), edge_iota(1)
    both = own_corner[...] + other_corner[...]
    diag = side[2 * EDGE : 2 * EDGE + 1]
    block = jnp.where(r > c, both, jnp.where(r < c, both.T, diag)) * inv_scale + loading()
    half = {"near": fine(lower, near)}
    block = block - fine(half["near"], half["near"], TURNED)
    right = steer_ref[pl.ds(0, EDGE), :].astype(jnp.float32)

    def forward(name, x):
        half[name] = fine(lower, x)

    def back(name, at):
        x = half[name]
        made_ref[:, at : at + x.shape[1]] = fine(lower, x, TURNED)

    def take(i, lhs, name, at):
        x = half[name]
        less_ref[i, :, at : at + x.shape[1]] = fine(half[lhs], x, TURNED)

    next_ref[...] = lower_inverse(
        block,
        [
            lambda: forward("far", far),
            lambda: forward("right", right),
            lambda: take(0, "near", "far", 0),
            lambda: take(1, "far", "far", 0),
            lambda: take(0, "near", "right", EDGE),
            lambda: take(1, "far", "right", EDGE),
            lambda: back("near", 0),
            lambda: back("far", EDGE),
            lambda: back("right", 2 * EDGE),
        ],
    )


def late_kernel(
    count_ref, own_late, other_late, own_side, other_side, steer_ref, made_ref, less_ref,
    lower_ref, out_ref,
):
    size, beams = steer_ref.shape
    inv_scale = inverse_scale(count_ref)
    diag = own_side[pl.ds(2 * EDGE, 8), :] + other_side[pl.ds(2 * EDGE, 8), :]
    near, block = unpack_late(own_late[...] + other_late[...], diag[1:2])
    near = near * inv_scale - less_ref[0, :, :EDGE]
    block = block * inv_scale + loading() - less_ref[1, :, :EDGE]
    lower = lower_ref[...]
    near = fine(lower, near)
    block = block - fine(near, near, TURNED)
    right = [
        steer_ref[pl.ds(i * EDGE, EDGE), :].astype(jnp.float32) - less_ref[i - 1, :, EDGE:]
        for i in (1, 2)
    ]
    made = made_ref[...]
    close, far, top = made[:, :EDGE], made[:, EDGE : 2 * EDGE], made[:, 2 * EDGE :]
    got = {}

    def forward():
        got["half"] = fine(lower, right[0])

    def last():
        got["last"] = right[1] - fine(near, got["half"], TURNED)

    def middle():
        got["middle"] = fine(lower, got["half"], TURNED)

    def step():
        got["step"] = fine(lower, near, TURNED)

    def base():
        got["base"] = jnp.concatenate([top - fine(close, got["middle"]), got["middle"]], axis=0)

    def turn():
        got["turn"] = jnp.concatenate([far - fine(close, got["step"]), got["step"]], axis=0)

    end = lower_inverse(block, [forward, last, middle, step, base, turn])
    x = fine(end, fine(end, got["last"]), TURNED)
    found = jnp.concatenate([got["base"] - fine(got["turn"], x), x], axis=0)
    response = jnp.sum(steer_ref[...].astype(jnp.float32) * found, axis=0, keepdims=True)
    out_ref[...] = (found * (1.0 / response)).astype(out_ref.dtype)


def make_weights(count, own, other, steering):
    size, beams = steering.shape
    smem = pl.BlockSpec(memory_space=pltpu.SMEM)
    vmem = pl.BlockSpec(memory_space=pltpu.VMEM)
    wide = EDGE + beams
    square = jax.ShapeDtypeStruct((EDGE, EDGE), jnp.float32)

    def call(kernel, out_shape, *args):
        return pl.pallas_call(
            kernel,
            out_shape=out_shape,
            in_specs=[smem] + [vmem] * len(args),
            out_specs=jax.tree.map(lambda _: vmem, out_shape),
            compiler_params=pltpu.CompilerParams(vmem_limit_bytes=VMEM_BYTES),
            cost_estimate=pl.CostEstimate(flops=10**9, bytes_accessed=10**6, transcendentals=0),
        )(count, *args)

    corner = call(corner_kernel, square, own[0], other[0])
    made, less, second = call(
        side_kernel,
        [
            jax.ShapeDtypeStruct((EDGE, EDGE + wide), jnp.float32),
            jax.ShapeDtypeStruct((2, EDGE, wide), jnp.float32),
            square,
        ],
        own[0], other[0], own[1], other[1], steering, corner,
    )
    return call(
        late_kernel,
        jax.ShapeDtypeStruct((size, beams), jnp.bfloat16),
        own[2], other[2], own[1], other[1], steering, made, less, second,
    )


def split_kernel(which_ref, x_ref, out_ref, sems):
    halves, group = x_ref.shape[:2]
    chunk = group // 4
    copies = []
    for s in range(halves):
        for i in range(4):
            part = pl.ds(i * chunk, chunk)
            copies.append(
                pltpu.make_async_copy(
                    x_ref.at[which_ref[s], part], out_ref.at[part, s], sems.at[s, i]
                )
            )
    for copy in copies:
        copy.start()
    for copy in copies:
        copy.wait()


def split(which, x):
    halves, group, rows, wide = x.shape
    return pl.pallas_call(
        split_kernel,
        out_shape=jax.ShapeDtypeStruct((group, halves, rows, wide), x.dtype),
        in_specs=[pl.BlockSpec(memory_space=pltpu.SMEM), pl.BlockSpec(memory_space=pltpu.HBM)],
        out_specs=pl.BlockSpec(memory_space=pltpu.VMEM),
        scratch_shapes=[pltpu.SemaphoreType.DMA((halves, 4))],
        compiler_params=pltpu.CompilerParams(vmem_limit_bytes=2 * VMEM_BYTES),
        cost_estimate=pl.CostEstimate(flops=0, bytes_accessed=2 * x.size, transcendentals=0),
    )(which, x)


def body(halves, snapshots, steering, train_list, train_count):
    bin_total, gate_rows, channels = snapshots.shape
    half = lax.axis_index("half").astype(jnp.int32)
    group = bin_total // halves
    order, base = jnp.stack([half, 1 - half]), half[None] * group
    peers = [(0, 1), (1, 0)]

    def exchange(x):
        return lax.all_to_all(x, INNER, split_axis=0, concat_axis=0, tiled=True)

    other_list = lax.ppermute(train_list, "half", peers)
    other_count = lax.ppermute(train_count, "half", peers)
    outgoing = split(order, snapshots.reshape(halves, group, gate_rows, channels))
    outgoing, other_list, other_count, base = lax.optimization_barrier(
        (outgoing, other_list, other_count, base)
    )
    blocks, train_list, train_count = lax.optimization_barrier(
        (exchange(outgoing), train_list, train_count)
    )

    other_gram = partial_gram(1, base, other_list, other_count, blocks)
    own_gram = partial_gram(0, base, train_list, train_count, blocks)
    last, own_gram = lax.optimization_barrier((other_gram[2], own_gram))
    arrived = [lax.ppermute(x, "half", peers) for x in (other_gram[0], other_gram[1], last)]
    weights = make_weights(train_count, own_gram, arrived, steering[0])
    other_weights = lax.ppermute(weights, "half", peers)

    def beams(x, w):
        made = jnp.einsum("ngd,de->nge", x, w, preferred_element_type=jnp.float32)
        return made.astype(jnp.bfloat16)

    made = jnp.stack([beams(blocks[:, 0], weights), beams(blocks[:, 1], other_weights)], axis=1)
    made, here, there = lax.optimization_barrier((made, half, 1 - half))
    out = jnp.moveaxis(exchange(made), 1, 0)
    sets = [
        lax.dynamic_index_in_dim(out, at, 0, keepdims=False, allow_negative_indices=False)
        for at in (here, there)
    ]
    return jnp.concatenate(sets, axis=0)


def solution(mesh):
    ranges, dopplers = mesh.devices.shape
    halves = 2
    cut = Mesh(mesh.devices.reshape(halves, ranges // halves, dopplers), EVERY)

    def run(*args):
        return body(halves, *args)

    return jax.shard_map(
        run,
        mesh=cut,
        in_specs=(P(None, EVERY, None), P(EVERY, None, None), P(EVERY, None), P(EVERY)),
        out_specs=P(None, EVERY, None),
        check_vma=False,
    )
```
